512 devices in a mesh: wide: 128 (over z_lo, x, y, core), narrow: 4 (over z_hi).
Axes of the slice: x: 4, y: 4, z: 16 (z_hi: 4, z_lo: 4; z = z_hi * 4 + z_lo), core: 2. Of those that a mesh axis runs over, the one named last changes fastest.
Arguments:
- grad_in: float32 [131072, 128], P(('wide', 'narrow')), may hold values from -6 to 6
- phi_slope: bfloat16 [131072, 128], P(('wide', 'narrow')), may hold values from 0.049804688 to 1
- activations: bfloat16 [131072, 128], P(('wide', 'narrow')), may hold values from -6 to 6
- weight: bfloat16 [128, 128], replicated, may hold values from -0.5 to 0.5
- local_tiles: bfloat16 [512, 8, 128, 128], P(('wide', 'narrow')), may hold values from -0.0625 to 0.0625
- local_rows: int32 [512, 8], P(('wide', 'narrow')), may hold values from 0 to 1, as said below
- local_cols: int32 [512, 8], P(('wide', 'narrow')), may hold values from 0 to 7, as said below
- local_count: int32 [512], P(('wide', 'narrow')), may hold values from 1 to 8, 3072 in all
- remote_tiles: bfloat16 [512, 112, 128, 128], P(('wide', 'narrow')), may hold values from -0.0625 to 0.0625
- remote_rows: int32 [512, 112], P(('wide', 'narrow')), may hold values from 0 to 1, as said below
- remote_cols: int32 [512, 112], P(('wide', 'narrow')), may hold values from 0 to 55, as said below
- remote_count: int32 [512], P(('wide', 'narrow')), may hold values from 1 to 112, 43008 in all
- send_list: int32 [512, 128, 56], P(('wide', 'narrow')), may hold values from 0 to 1023
Outputs:
- adjoint: float32 [131072, 128], P(('wide', 'narrow'))
- weight_grad: float32 [128, 128], replicated
The draws below stay inside these ranges and needn't reach their ends.
Inputs may be any that keep to these rules, and one draw needn't show every extreme that they name: `local_count`: each device's live local tile slots; slots from this count onward are ignored, and some device uses all 8. `remote_count`: each device's live remote tile slots; slots from this count onward are ignored, and some device uses all 112. On one device no two local slots have the same pair of local_rows and local_cols. `local_cols`: see local_rows. On one device no two remote slots have the same pair of remote_rows and remote_cols. `remote_cols`: see remote_rows.
All inputs are finite; a program needn't handle non-finite values.
Results may differ from the reference program's by a relative error of at most 0.0031.
Values may be sent and summed in bfloat16 or wider, within the bound.
A program may use at most 64 MiB of HBM per device.

```python
import math
import jax
import jax.numpy as jnp
import numpy as np
from jax import lax

H = 128
TB = 128
NB = 2
ITERS = 2
LOC_PER = 4
HB = 56
REM_PER = 56
SENDN = 56
LT = 8
RT = 112
NODES = 131072
N_WIDE = 128
N_NARROW = 4
DEVICES = 512


def distinct_pairs(key, salt, col_range, slots):
    keys = jax.random.split(jax.random.fold_in(key, salt), DEVICES)
    total = NB * col_range

    def one_device(k):
        return jax.random.permutation(k, total)[:slots].astype(jnp.int32)
    return jax.vmap(one_device)(keys)


def draw_local_rows(key, part):
    return distinct_pairs(key, 11, N_NARROW * NB, LT) // (N_NARROW * NB)


def draw_local_cols(key, part):
    return distinct_pairs(key, 11, N_NARROW * NB, LT) % (N_NARROW * NB)


def draw_remote_rows(key, part):
    return distinct_pairs(key, 23, HB, RT) // HB


def draw_remote_cols(key, part):
    return distinct_pairs(key, 23, HB, RT) % HB


def place_ends(array, own_key, low, top_value):
    longest = array.shape.index(max(array.shape))
    spots = []
    for shift in (0, 1):
        where = [jax.random.randint(jax.random.fold_in(own_key, axis), (), 0, length) for axis, length in enumerate(array.shape)]
        where[longest] = (where[longest] + shift) % array.shape[longest]
        spots.append(tuple(where))
    return array.at[spots[0]].set(low).at[spots[1]].set(top_value)


def block_levels(stream_key, dims, cuts, least, high):
    def one(dim, parts):
        heights = jax.random.uniform(jax.random.fold_in(jax.random.fold_in(stream_key, 6), dim), (parts,), jnp.float32, least / len(cuts), high / len(cuts))
        return jnp.repeat(jnp.exp(heights), dims[dim] // parts).reshape((-1,) + (1,) * (len(dims) - dim - 1))

    factor_of = one(*cuts[0])
    for cut in cuts[1:]:
        factor_of = factor_of * one(*cut)
    return factor_of


def length_profile(amount, total, bound, skew):
    loads = [(1 << 20) // math.isqrt(grade ** skew) + 1 for grade in range(2, amount + 1)]
    spare, counts = total - bound - (amount - 1), [1] * (amount - 1)
    while spare > 0:
        candidates = [i for i in range(amount - 1) if counts[i] < bound]
        whole, budget = sum([loads[i] for i in candidates]), spare
        for i in candidates:
            more = min(bound - counts[i], max(1, budget * loads[i] // whole), spare)
            counts[i] = counts[i] + more
            spare = spare - more
    return np.array([bound] + counts)


def uneven_parts(rng, number_of, total, most, lean):
    if number_of == 2:
        one = jax.random.randint(rng, (), max(1, total - most), min(most, total - 1) + 1)
        return jnp.stack([one, total - one])
    sizes = jnp.asarray(length_profile(number_of, total, most, lean), jnp.int32)
    pairs = (number_of - 1) // 2
    source_of, taker = sizes[1:1 + 2 * pairs:2], sizes[2:2 + 2 * pairs:2]
    room = jnp.minimum(source_of - 1, most - taker)
    moved = jax.random.randint(jax.random.fold_in(rng, 1), (pairs,), 0, 1 << 20) % (room + 1)
    sizes = sizes.at[1:1 + 2 * pairs:2].set(source_of - moved).at[2:2 + 2 * pairs:2].set(taker + moved)
    return sizes[jax.random.permutation(jax.random.fold_in(rng, 2), number_of)]


def noise(own_key, dims, width, bound, cuts=(), kind=jnp.bfloat16):
    factor_of = block_levels(own_key, dims, cuts, -0.22, 0.18) if cuts else 1.0
    array = jax.random.normal(own_key, dims, jnp.float32) * width * factor_of
    return jnp.minimum(jnp.maximum(array, -bound), bound).astype(kind)


def setup_inputs(seed: int = 0) -> dict:
    splits = jax.random.split(jax.random.key(seed), 14)
    grad_in = noise(splits[0], (NODES, H), 1.0, 6.0, ((0, 512),), jnp.float32)
    phi_slope = jnp.clip(0.049804688 + 0.9501953 * jax.random.uniform(splits[1], (NODES, H), jnp.float32) ** block_levels(splits[1], (NODES, H), ((0, 512),), -0.2, 0.2), 0.049804688, 1.0).astype(jnp.bfloat16)
    activations = noise(splits[2], (NODES, H), 1.0, 6.0, ((0, 512),))
    weight = noise(splits[3], (H, H), H ** -0.5, 0.5)
    local_tiles = noise(splits[4], (DEVICES, LT, TB, TB), ((LOC_PER + REM_PER) * TB) ** -0.5, 0.0625, ((0, 512),))
    local_rows = draw_local_rows(jax.random.fold_in(splits[13], 71), 0)
    local_cols = draw_local_cols(jax.random.fold_in(splits[13], 71), 0)
    local_count = uneven_parts(splits[7], DEVICES, DEVICES * LT * 3 // 4, LT, 2).astype(jnp.int32)
    remote_tiles = noise(splits[8], (DEVICES, RT, TB, TB), ((LOC_PER + REM_PER) * TB) ** -0.5, 0.0625, ((0, 512),))
    remote_rows = draw_remote_rows(jax.random.fold_in(splits[13], 71), 0)
    remote_cols = draw_remote_cols(jax.random.fold_in(splits[13], 71), 0)
    remote_count = uneven_parts(splits[11], DEVICES, DEVICES * RT * 3 // 4, RT, 2).astype(jnp.int32)
    send_list = place_ends(jax.random.randint(splits[12], (DEVICES, N_WIDE, SENDN), 0, N_NARROW * NB * TB), jax.random.fold_in(splits[12], 1), 0, (N_NARROW * NB * TB) - 1).astype(jnp.int32)
    return {"grad_in": grad_in, "phi_slope": phi_slope, "activations": activations, "weight": weight, "local_tiles": local_tiles, "local_rows": local_rows, "local_cols": local_cols, "local_count": local_count, "remote_tiles": remote_tiles, "remote_rows": remote_rows, "remote_cols": remote_cols, "remote_count": remote_count, "send_list": send_list}


GAMMA = 0.5

def tile_product(tile_values, row_ids, col_ids, live_count, sources):
    slot_count = row_ids.shape[0]
    picked = sources[col_ids]
    product = jnp.einsum('kij,kjh->kih', tile_values.astype(jnp.float32), picked.astype(jnp.float32))
    is_live = jnp.arange(slot_count, dtype=jnp.int32) < live_count
    row_table = ((row_ids[None, :] == jnp.arange(NB, dtype=jnp.int32)[:, None]) & is_live[None, :]).astype(jnp.float32)
    summed = jnp.einsum('rk,kih->rih', row_table, product, precision=lax.Precision.HIGHEST)
    return summed.reshape(NB * TB, H)

def reference(grad_in, phi_slope, activations, weight, local_tiles, local_rows, local_cols, local_count, remote_tiles, remote_rows, remote_cols, remote_count, send_list):
    dev_rows = NB * TB
    outgoing = send_list.reshape(N_WIDE, N_NARROW, N_WIDE, SENDN)
    offsets = (jnp.arange(N_WIDE, dtype=jnp.int32) * (N_NARROW * dev_rows))[:, None, None, None]
    halo_index = jnp.transpose(outgoing + offsets, (2, 1, 0, 3)).reshape(N_WIDE * N_NARROW, N_WIDE * SENDN)
    adjoint = grad_in
    for iteration in range(ITERS):
        mapped = jnp.dot(adjoint.astype(jnp.bfloat16), weight.T, preferred_element_type=jnp.float32)
        message = (mapped * phi_slope.astype(jnp.float32)).astype(jnp.bfloat16)

        def per_device(device):
            start = (device // N_NARROW * (N_NARROW * dev_rows)).astype(jnp.int32)
            gathered = lax.dynamic_slice_in_dim(message, start, N_NARROW * dev_rows, 0).reshape(N_NARROW * NB, TB, H)
            halo_blocks = message[halo_index[device]].reshape(HB, TB, H)
            near = tile_product(local_tiles[device], local_rows[device], local_cols[device], local_count[device], gathered)
            far = tile_product(remote_tiles[device], remote_rows[device], remote_cols[device], remote_count[device], halo_blocks)
            return near + far
        spread = lax.map(per_device, jnp.arange(N_WIDE * N_NARROW, dtype=jnp.int32)).reshape(NODES, H)
        adjoint = grad_in + GAMMA * spread
    summed = lax.dot_general(activations, adjoint.astype(jnp.bfloat16), (((0,), (0,)), ((), ())), preferred_element_type=jnp.float32)
    weight_grad = summed * (GAMMA / jnp.sqrt(jnp.float32(NODES)))
    return (adjoint, weight_grad)
```

```python
import functools
import math

import jax
import jax.numpy as jnp
from jax import lax
from jax.experimental import pallas as pl
from jax.experimental.pallas import tpu as pltpu
from jax.sharding import PartitionSpec as P

ITERS = 2
GAMMA = 0.5
Z_LO = 4
CORES = 2
MESH = pl.DeviceIdType.MESH
F32 = jnp.float32
BF16 = jnp.bfloat16


def loop(count, body, start=0):
    def step(i, carry):
        body(i)
        return carry

    lax.fori_loop(start, count, step, 0)


def kernel(
    cfg,
    slot_of,
    grad_ref,
    phi_ref,
    act_ref,
    weight_ref,
    list_ref,
    local_hbm,
    remote_hbm,
    adj_ref,
    wg_ref,
    tiles,
    table,
    lists,
    index,
    picked,
    send,
    recv,
    halo,
    total,
    part,
    plane_sum,
    column_sum,
    wg_all,
    tile_sem,
    list_send,
    list_recv,
    ring_send,
    ring_recv,
    swap_send,
    swap_recv,
    plane_send,
    plane_recv,
    column_send,
    column_recv,
    last_send,
    last_recv,
):
    plane, narrow, rows, tb, sendn, batch, scale = cfg
    depth = Z_LO * narrow
    chips = plane // CORES
    half = rows // 2
    steps = depth // 2
    hidden = grad_ref.shape[1]
    n_local, n_remote = local_hbm.shape[0], remote_hbm.shape[0]
    zero_slot = n_local + n_remote
    blocks = rows // tb
    group_blocks = narrow * blocks
    halo_blocks = halo.shape[0] // tb

    wide_at, narrow_at = lax.axis_index("wide"), lax.axis_index("narrow")
    low, me = wide_at // plane, lax.rem(wide_at, plane)
    z = narrow_at * Z_LO + low
    core = lax.rem(me, CORES)
    chip = me // CORES

    def in_plane(other):
        return (low * plane + other, narrow_at)

    def in_column(other):
        return (lax.rem(other, Z_LO) * plane + me, other // Z_LO)

    def ahead(k):
        return lax.rem(me + k, plane)

    def behind(k):
        return lax.rem(me + plane - k, plane)

    barrier = pltpu.get_barrier_semaphore()

    def greet_plane(k):
        pl.semaphore_signal(barrier, inc=1, device_id=in_plane(ahead(k)), device_id_type=MESH)

    def greet_column(k):
        pl.semaphore_signal(barrier, inc=1, device_id=in_column(lax.rem(z + k, depth)), device_id_type=MESH)

    loop(plane, greet_plane, 1)
    loop(depth, greet_column, 1)

    near_tiles = pltpu.make_async_copy(local_hbm, tiles.at[pl.ds(0, n_local)], tile_sem.at[0])
    far_tiles = pltpu.make_async_copy(remote_hbm, tiles.at[pl.ds(n_local, n_remote)], tile_sem.at[1])
    near_tiles.start()
    far_tiles.start()
    tiles[zero_slot] = jnp.zeros((tb, tb), BF16)

    def make_message(it, adjoint):
        mapped = lax.dot_general(
            adjoint.astype(BF16), weight_ref[...], (((1,), (1,)), ((), ())), preferred_element_type=F32
        )
        message = (mapped * phi_ref[...].astype(F32)).astype(BF16)
        table[it, low, pl.ds(pl.multiple_of(narrow_at * rows, rows), rows), :] = message

    make_message(0, grad_ref[...])
    lists[low] = list_ref[pl.ds(pl.multiple_of(low * plane, 8), plane), :]

    pl.semaphore_wait(barrier, plane - 1 + depth - 1)

    def list_copy(k):
        other = lax.rem(low + k, Z_LO)
        return pltpu.make_async_remote_copy(
            src_ref=list_ref.at[pl.ds(pl.multiple_of(other * plane, 8), plane)],
            dst_ref=lists.at[low],
            send_sem=list_send.at[k],
            recv_sem=list_recv.at[k],
            device_id=(other * plane + me, narrow_at),
            device_id_type=MESH,
        )

    def ring_copy(it, way, step, piece):
        owner = lax.rem(z + (depth - step if way == 0 else step), depth)
        at = pl.multiple_of(owner // Z_LO * rows + piece * half, half)
        ref = table.at[it, lax.rem(owner, Z_LO), pl.ds(at, half)]
        return pltpu.make_async_remote_copy(
            src_ref=ref,
            dst_ref=ref,
            send_sem=ring_send.at[it, way, step, piece],
            recv_sem=ring_recv.at[it, way, step, piece],
            device_id=in_column(lax.rem(z + (1 if way == 0 else depth - 1), depth)),
            device_id_type=MESH,
        )

    def ring_hops():
        for step in range(steps):
            for piece in range(2):
                for way in range(2):
                    if step < steps - 1 or piece == way:
                        yield way, step, piece

    def make_index(source):
        turned = jnp.transpose(lists[source])
        for k in range(plane):
            index[k, source * sendn : (source + 1) * sendn, :] = jnp.broadcast_to(turned[:, k : k + 1], (sendn, 128))

    def gather_column(it):
        for way, step, piece in ring_hops():
            if step == 0:
                ring_copy(it, way, 0, piece).start()

        @pl.when(it == 0)
        def _():
            loop(Z_LO, lambda k: list_copy(k).start(), 1)

        for way, step, piece in ring_hops():
            ring_copy(it, way, step, piece).wait_recv()
            if step < steps - 2 or (step == steps - 2 and piece == way):
                ring_copy(it, way, step + 1, piece).start()
            if step == 0 and way == 1 and piece == 1:

                @pl.when(it == 0)
                def _():
                    loop(Z_LO, lambda k: list_copy(k).wait(), 1)
                    for source in range(Z_LO):
                        make_index(source)

        for way, step, piece in ring_hops():
            ring_copy(it, way, step, piece).wait_send()

    def swap_copy(it, k):
        return pltpu.make_async_remote_copy(
            src_ref=send.at[it, k],
            dst_ref=recv.at[it, k],
            send_sem=swap_send.at[it, k],
            recv_sem=swap_recv.at[it, k],
            device_id=in_plane(ahead(k)),
            device_id_type=MESH,
        )

    group_rows = narrow * rows

    def send_batch(it, first):
        def select(source):
            wanted = jnp.concatenate(
                [index[ahead(first + j), pl.ds(pl.multiple_of(source * sendn, 8), sendn), :] for j in range(batch)], axis=0
            )
            lane = lax.broadcasted_iota(jnp.int32, wanted.shape, 1)
            hot = jnp.concatenate(
                [jnp.where(wanted == lane + at, 1.0, 0.0).astype(BF16) for at in range(0, group_rows, 128)], axis=1
            )
            got = jnp.dot(hot, table[it, source], preferred_element_type=F32)
            for j in range(batch):
                picked[j, pl.ds(pl.multiple_of(source * sendn, 8), sendn), :] = got[j * sendn : (j + 1) * sendn]

        loop(Z_LO, select)

        def post(j):
            send[it, first + j] = picked[j].astype(BF16)

            @pl.when(first + j > 0)
            def _():
                swap_copy(it, first + j).start()

        loop(batch, post)

    def place(it, k, ref):
        got = ref[it, k].astype(F32)
        for source in range(Z_LO):
            at = pl.multiple_of((source * plane + behind(k)) * sendn, 8)
            halo[pl.ds(at, sendn), :] = got[source * sendn : (source + 1) * sendn]

    def tile_pair(base, per_row, c):
        top = jnp.concatenate([tiles[slot_of[base + c]], tiles[slot_of[base + c + 1]]], axis=1)
        low_row = jnp.concatenate(
            [tiles[slot_of[base + per_row + c]], tiles[slot_of[base + per_row + c + 1]]], axis=1
        )
        return jnp.concatenate([top, low_row], axis=0)

    def iterate(it):
        gather_column(it)
        loop(plane // batch, lambda c: send_batch(it, c * batch))
        place(it, 0, send)

        @pl.when(it == 0)
        def _():
            near_tiles.wait()
            far_tiles.wait()

        total[...] = jnp.zeros_like(total)

        def near(c):
            source = table[it, low, pl.ds(pl.multiple_of(c * 2 * tb, tb), 2 * tb), :]
            total[...] += jnp.dot(tile_pair(0, group_blocks, 2 * c), source, preferred_element_type=F32)

        loop(group_blocks // 2, near)

        def receive(k):
            swap_copy(it, k).wait_recv()
            place(it, k, recv)

        loop(plane, receive, 1)

        def far(c):
            source = halo[pl.ds(pl.multiple_of(c * 2 * tb, tb), 2 * tb), :].astype(BF16)
            total[...] += jnp.dot(
                tile_pair(blocks * group_blocks, halo_blocks, 2 * c), source, preferred_element_type=F32
            )

        loop(halo_blocks // 2, far)
        loop(plane, lambda k: swap_copy(it, k).wait_send(), 1)
        adj_ref[...] = grad_ref[...] + GAMMA * total[...]

        @pl.when(it < ITERS - 1)
        def _():
            make_message(it + 1, adj_ref[...])

    loop(ITERS, iterate)

    gradient = lax.dot_general(
        act_ref[...], adj_ref[...].astype(BF16), (((0,), (0,)), ((), ())), preferred_element_type=F32
    )
    piece_rows = hidden // chips
    for j in range(chips):
        part[j] = gradient[j * piece_rows : (j + 1) * piece_rows]

    def plane_copy(k):
        return pltpu.make_async_remote_copy(
            src_ref=part.at[ahead(k) // CORES],
            dst_ref=plane_sum.at[me],
            send_sem=plane_send.at[k],
            recv_sem=plane_recv.at[k],
            device_id=in_plane(ahead(k)),
            device_id_type=MESH,
        )

    loop(plane, lambda k: plane_copy(k).start(), 1)
    plane_sum[me] = part[chip]
    loop(plane, lambda k: plane_copy(k).wait(), 1)
    column_sum[z] = jnp.sum(plane_sum[...], axis=0)

    def column_copy(k):
        return pltpu.make_async_remote_copy(
            src_ref=column_sum.at[z],
            dst_ref=column_sum.at[z],
            send_sem=column_send.at[k],
            recv_sem=column_recv.at[k],
            device_id=in_column(lax.rem(z + k, depth)),
            device_id_type=MESH,
        )

    loop(depth, lambda k: column_copy(k).start(), 1)
    loop(depth, lambda k: column_copy(k).wait(), 1)
    wg_all[chip] = jnp.sum(column_sum[...], axis=0) * scale

    def last_copy(k):
        return pltpu.make_async_remote_copy(
            src_ref=wg_all.at[chip],
            dst_ref=wg_all.at[chip],
            send_sem=last_send.at[k],
            recv_sem=last_recv.at[k],
            device_id=in_plane(ahead(k * CORES)),
            device_id_type=MESH,
        )

    loop(chips, lambda k: last_copy(k).start(), 1)
    loop(chips, lambda k: last_copy(k).wait(), 1)
    wg_ref[...] = wg_all[...]


def slot_table(local_rows, local_cols, local_count, remote_rows, remote_cols, remote_count, blocks, group_blocks, halo_blocks):
    n_local, n_remote = local_rows.shape[0], remote_rows.shape[0]
    near = jnp.where(jnp.arange(n_local) < local_count, local_rows * group_blocks + local_cols, -1)
    far = jnp.where(
        jnp.arange(n_remote) < remote_count, blocks * group_blocks + remote_rows * halo_blocks + remote_cols, -1
    )
    keys = jnp.concatenate([near, far])
    none = n_local + n_remote
    pairs = jnp.arange(blocks * (group_blocks + halo_blocks), dtype=jnp.int32)
    slots = jnp.arange(none, dtype=jnp.int32)
    return none + jnp.sum(jnp.where(keys[None, :] == pairs[:, None], slots[None, :] - none, 0), axis=1)


def per_device(
    grad_in,
    phi_slope,
    activations,
    weight,
    local_tiles,
    local_rows,
    local_cols,
    local_count,
    remote_tiles,
    remote_rows,
    remote_cols,
    remote_count,
    send_list,
):
    wide, narrow = lax.axis_size("wide"), lax.axis_size("narrow")
    plane = wide // Z_LO
    chips = plane // CORES
    depth = Z_LO * narrow
    rows, hidden = grad_in.shape
    tb = local_tiles.shape[2]
    sendn = send_list.shape[2]
    n_local, n_remote = local_tiles.shape[1], remote_tiles.shape[1]
    blocks, group_blocks, halo_blocks = rows // tb, narrow * rows // tb, wide * sendn // tb
    batch = math.gcd(plane, 8)
    scale = GAMMA / math.sqrt(rows * wide * narrow)
    slot_of = slot_table(
        local_rows[0], local_cols[0], local_count[0], remote_rows[0], remote_cols[0], remote_count[0],
        blocks, group_blocks, halo_blocks,
    )
    vmem = pl.BlockSpec(memory_space=pltpu.VMEM)
    anywhere = pl.BlockSpec(memory_space=pl.ANY)
    piece = (hidden // chips, hidden)
    per_dest = Z_LO * sendn
    dma = pltpu.SemaphoreType.DMA
    adjoint, weight_grad = pl.pallas_call(
        functools.partial(kernel, (plane, narrow, rows, tb, sendn, batch, scale)),
        out_shape=(
            jax.ShapeDtypeStruct((rows, hidden), F32),
            jax.ShapeDtypeStruct((chips,) + piece, F32),
        ),
        in_specs=[pl.BlockSpec(memory_space=pltpu.SMEM)] + [vmem] * 5 + [anywhere] * 2,
        out_specs=(vmem, vmem),
        scratch_shapes=[
            pltpu.VMEM((n_local + n_remote + 1, tb, tb), BF16),
            pltpu.VMEM((ITERS, Z_LO, narrow * rows, hidden), BF16),
            pltpu.VMEM((Z_LO, plane, sendn), jnp.int32),
            pltpu.VMEM((plane, per_dest, 128), jnp.int32),
            pltpu.VMEM((batch, per_dest, hidden), F32),
            pltpu.VMEM((ITERS, plane, per_dest, hidden), BF16),
            pltpu.VMEM((ITERS, plane, per_dest, hidden), BF16),
            pltpu.VMEM((wide * sendn, hidden), F32),
            pltpu.VMEM((rows, hidden), F32),
            pltpu.VMEM((chips,) + piece, F32),
            pltpu.VMEM((plane,) + piece, F32),
            pltpu.VMEM((depth,) + piece, F32),
            pltpu.VMEM((chips,) + piece, F32),
            dma((2,)),
            dma((Z_LO,)),
            dma((Z_LO,)),
            dma((ITERS, 2, depth // 2, 2)),
            dma((ITERS, 2, depth // 2, 2)),
            dma((ITERS, plane)),
            dma((ITERS, plane)),
            dma((plane,)),
            dma((plane,)),
            dma((depth,)),
            dma((depth,)),
            dma((chips,)),
            dma((chips,)),
        ],
        compiler_params=pltpu.CompilerParams(
            collective_id=0, has_side_effects=True, vmem_limit_bytes=48 * 1024 * 1024
        ),
    )(slot_of, grad_in, phi_slope, activations, weight, send_list[0], local_tiles[0], remote_tiles[0])
    return adjoint, weight_grad.reshape(hidden, hidden)


def solution(mesh):
    placed = (
        P(("wide", "narrow"), None),
        P(("wide", "narrow"), None),
        P(("wide", "narrow"), None),
        P(),
        P(("wide", "narrow"), None, None, None),
        P(("wide", "narrow"), None),
        P(("wide", "narrow"), None),
        P(("wide", "narrow")),
        P(("wide", "narrow"), None, None, None),
        P(("wide", "narrow"), None),
        P(("wide", "narrow"), None),
        P(("wide", "narrow")),
        P(("wide", "narrow"), None, None),
    )
    return jax.shard_map(
        per_device,
        mesh=mesh,
        in_specs=placed,
        out_specs=(P(("wide", "narrow"), None), P()),
        check_vma=False,
    )
```

```python
import functools
import math

import jax
import jax.numpy as jnp
from jax import lax
from jax.experimental import pallas as pl
from jax.experimental.pallas import tpu as pltpu
from jax.sharding import PartitionSpec as P

ITERS = 2
GAMMA = 0.5
Z_LO = 4
CORES = 2
MESH = pl.DeviceIdType.MESH
F32 = jnp.float32
BF16 = jnp.bfloat16


def loop(count, body, start=0):
    def step(i, carry):
        body(i)
        return carry

    lax.fori_loop(start, count, step, 0)


def kernel(
    cfg,
    local_count,
    remote_count,
    grad_hbm,
    phi_hbm,
    act_hbm,
    weight_hbm,
    list_hbm,
    local_hbm,
    remote_hbm,
    local_rows,
    local_cols,
    remote_rows,
    remote_cols,
    adj_ref,
    wg_ref,
    grad_ref,
    phi_ref,
    act_ref,
    weight_ref,
    list_ref,
    tiles,
    local_at,
    remote_at,
    slot_rows,
    slot_of,
    table,
    lists,
    index,
    send,
    halo,
    total,
    part,
    plane_sum,
    near_sum,
    low_sum,
    wg_all,
    in_sem,
    slot_sem,
    list_send,
    list_recv,
    group_send,
    group_recv,
    twin_send,
    twin_recv,
    swap_send,
    swap_recv,
    plane_send,
    plane_recv,
    near_send,
    near_recv,
    low_send,
    low_recv,
    last_send,
    last_recv,
):
    plane, narrow, rows, tb, sendn, batch, scale = cfg
    depth = Z_LO * narrow
    chips = plane // CORES
    side = math.isqrt(chips)
    count = Z_LO * chips
    per_chip = CORES * sendn
    hidden = grad_ref.shape[1]
    n_local, n_remote = local_hbm.shape[0], remote_hbm.shape[0]
    zero_slot = n_local + n_remote
    blocks = rows // tb
    group_rows = narrow * rows
    group_blocks = narrow * blocks
    layer_blocks = chips * per_chip // tb
    halo_blocks = Z_LO * layer_blocks
    span = math.gcd(layer_blocks, 7)

    wide_at, m = lax.axis_index("wide"), lax.axis_index("narrow")
    low, me = wide_at // plane, lax.rem(wide_at, plane)
    z = m * Z_LO + low
    core, chip = lax.rem(me, CORES), me // CORES
    twin = me + 1 - 2 * core
    even = lax.rem(low, 2) == 0

    def device(z_at, in_plane):
        return (lax.rem(z_at, Z_LO) * plane + in_plane, z_at // Z_LO)

    def offset(k):
        phase, inner = k // (count // 2), lax.rem(k, count // 2)
        turn, j = lax.rem(inner, 2), inner // 2
        i_x = j // side
        i_y = lax.rem(j, side)

        def far_first(i):
            if side == 1:
                return 0 * i
            return jnp.where(i == 0, 2, jnp.where(i == 1, 1, jnp.where(i == 2, 3, 0)))

        dx, dy = far_first(i_x), far_first(i_y)
        dx = jnp.where(turn == 0, dx, lax.rem(side - dx, side))
        dy = jnp.where(turn == 0, dy, lax.rem(side - dy, side))
        two = jnp.where(even, 2, depth - 2)
        dz = jnp.where(phase == 0, jnp.where(turn == 0, two, 0), jnp.where(turn == 0, 1, depth - 1))
        return dz, dx, dy

    self_k = count // 2 - 1

    def target(k, back=False):
        dz, dx, dy = offset(k)
        if back:
            dz, dx, dy = depth - dz, side - dx, side - dy
        x, y = lax.rem(chip // side + dx, side), lax.rem(lax.rem(chip, side) + dy, side)
        return lax.rem(z + dz, depth), x * side + y

    def partners(body):
        loop(self_k, body)
        loop(count, body, self_k + 1)

    barrier = pltpu.get_barrier_semaphore()

    def greet(where):
        pl.semaphore_signal(barrier, inc=1, device_id=where, device_id_type=MESH)

    def greet_source(k):
        z_at, chip_at = target(k, back=True)
        greet(device(z_at, chip_at * CORES + core))

    def greet_group(k):
        z_at = lax.rem(z + Z_LO * k, depth)
        greet(device(z_at, me))
        greet(device(z_at, twin))

    loop(narrow, greet_group, 1)
    greet(device(z, twin))
    partners(greet_source)

    inputs = [
        (grad_hbm, grad_ref),
        (phi_hbm, phi_ref),
        (weight_hbm, weight_ref),
        (list_hbm, list_ref),
        (local_rows, local_at.at[0:1]),
        (local_cols, local_at.at[1:2]),
        (remote_rows, remote_at.at[0:1]),
        (remote_cols, remote_at.at[1:2]),
        (local_hbm, tiles.at[pl.ds(0, n_local)]),
        (remote_hbm, tiles.at[pl.ds(n_local, n_remote)]),
        (act_hbm, act_ref),
    ]
    inputs = [pltpu.make_async_copy(src, dst, in_sem.at[i]) for i, (src, dst) in enumerate(inputs)]
    for copy in inputs:
        copy.start()

    def make_message(it, adjoint):
        mapped = lax.dot_general(
            adjoint.astype(BF16), weight_ref[...], (((1,), (1,)), ((), ())), preferred_element_type=F32
        )
        message = (mapped * phi_ref[...].astype(F32)).astype(BF16)
        table[it, core, pl.ds(pl.multiple_of(m * rows, rows), rows), :] = message

    for copy in inputs[:3]:
        copy.wait()
    make_message(0, grad_ref[...])
    inputs[3].wait()
    pl.semaphore_wait(barrier, 2 * (narrow - 1) + 1 + count - 1)

    def group_block(it, g, k):
        at = pl.multiple_of(lax.rem(m + narrow - k, narrow) * rows, rows)
        return table.at[it, g, pl.ds(at, rows)]

    def group_copy(it, k):
        return pltpu.make_async_remote_copy(
            src_ref=group_block(it, core, 0),
            dst_ref=group_block(it, core, 0),
            send_sem=group_send.at[it, k],
            recv_sem=group_recv.at[it, k],
            device_id=device(lax.rem(z + Z_LO * k, depth), me),
            device_id_type=MESH,
        )

    def twin_copy(it, k):
        return pltpu.make_async_remote_copy(
            src_ref=group_block(it, core, k),
            dst_ref=group_block(it, core, k),
            send_sem=twin_send.at[it, k],
            recv_sem=twin_recv.at[it, k],
            device_id=device(z, twin),
            device_id_type=MESH,
        )

    away = jnp.where(low < Z_LO // 2, Z_LO - 1, 0)
    stay = jnp.where(low < Z_LO // 2, 0, plane)
    holder = lax.rem(z + jnp.where(low < Z_LO // 2, Z_LO, depth - Z_LO), depth)
    away_rows = pl.ds(pl.multiple_of(away * plane, 8), plane)
    stay_rows = pl.ds(pl.multiple_of(stay, 8), (Z_LO - 1) * plane)

    def list_copies():
        for i, (part_rows, where) in enumerate(
            ((away_rows, device(holder, me)), (away_rows, device(holder, twin)), (stay_rows, device(z, twin)))
        ):
            yield pltpu.make_async_remote_copy(
                src_ref=list_ref.at[part_rows],
                dst_ref=lists.at[core, part_rows],
                send_sem=list_send.at[i],
                recv_sem=list_recv.at[i],
                device_id=where,
                device_id_type=MESH,
            )

    def make_index(g, b):
        turned = jnp.transpose(lists[g, pl.ds(b * plane + core, chips, stride=CORES), :])
        for c in range(chips):
            index[b * chips + c, g * sendn : (g + 1) * sendn, :] = jnp.broadcast_to(turned[:, c : c + 1], (sendn, 128))

    def make_slots():
        def row_of(at, alive, per_row, first):
            key = at[0:1] * per_row + at[1:2]
            slot = lax.broadcasted_iota(jnp.int32, key.shape, 1)
            key = jnp.where(slot < alive, key, -1)
            wide_key = jnp.broadcast_to(key, (128, key.shape[1]))
            pair = lax.broadcasted_iota(jnp.int32, wide_key.shape, 0)
            value = lax.broadcasted_iota(jnp.int32, wide_key.shape, 1) + (first - zero_slot)
            found = zero_slot + jnp.sum(jnp.where(wide_key == pair, value, 0), axis=1, keepdims=True)
            return jnp.transpose(jnp.broadcast_to(found, (128, 128)))[0:1]

        slot_rows[0:1] = row_of(local_at[...], local_count[0], group_blocks, 0)
        slot_rows[1:2] = row_of(remote_at[...], remote_count[0], halo_blocks, n_local)
        copy = pltpu.make_async_copy(slot_rows, slot_of, slot_sem)
        copy.start()
        copy.wait()

    def gather_group(it):
        far_first = sorted(range(1, narrow), key=lambda k: -min(k, narrow - k))
        for k in far_first:
            group_copy(it, k).start()
        twin_copy(it, 0).start()

        @pl.when(it == 0)
        def _():
            for copy in list_copies():
                copy.start()
            lists[core, stay_rows, :] = list_ref[stay_rows, :]
            for copy in inputs[4:8]:
                copy.wait()
            tiles[zero_slot] = jnp.zeros((tb, tb), BF16)
            make_slots()

        for i, k in enumerate(reversed(far_first)):
            group_copy(it, k).wait_recv()
            twin_copy(it, k).start()
            if i == 0:

                @pl.when(it == 0)
                def _():
                    for copy in list_copies():
                        copy.wait()
                    for g in range(CORES):
                        for b in range(Z_LO):
                            make_index(g, b)

        for k in range(narrow):
            twin_copy(it, k).wait_recv()

    my_rows = pl.ds(pl.multiple_of((low * chips + chip) * per_chip, 16), per_chip)

    def swap_copy(it, k):
        z_at, chip_at = target(k)
        return pltpu.make_async_remote_copy(
            src_ref=send.at[it, k],
            dst_ref=halo.at[it, my_rows],
            send_sem=swap_send.at[it, k],
            recv_sem=swap_recv.at[it, k],
            device_id=device(z_at, chip_at * CORES + core),
            device_id_type=MESH,
        )

    def send_batch(it, first):
        wanted = []
        for j in range(batch):
            z_at, chip_at = target(first + j)
            wanted.append(lax.rem(z_at, Z_LO) * chips + chip_at)

        def select(g):
            want = jnp.concatenate([index[w, g * sendn : (g + 1) * sendn, :] for w in wanted], axis=0)
            lane = lax.broadcasted_iota(jnp.int32, want.shape, 1)
            hot = jnp.concatenate(
                [jnp.where(want == lane + at, 1.0, 0.0).astype(BF16) for at in range(0, group_rows, 128)], axis=1
            )
            return jnp.dot(hot, table[it, g], preferred_element_type=F32)

        got = [select(g) for g in range(CORES)]
        for j in range(batch):
            both = jnp.concatenate([rows_of[j * sendn : (j + 1) * sendn] for rows_of in got], axis=0)
            send[it, first + j] = both.astype(BF16)

        def post(j):
            @pl.when(first + j != self_k)
            def _():
                swap_copy(it, first + j).start()

        loop(batch, post)

    def tile_rows(kind, per_row, first, width):
        return jnp.concatenate(
            [
                jnp.concatenate([tiles[slot_of[kind, r * per_row + first + c]] for c in range(width)], axis=1)
                for r in range(blocks)
            ],
            axis=0,
        )

    def layer(it, b):
        def some(i):
            first = b * layer_blocks + i * span
            source = halo[it, pl.ds(pl.multiple_of(first * tb, tb), span * tb), :]
            total[...] += jnp.dot(tile_rows(1, halo_blocks, first, span), source, preferred_element_type=F32)

        loop(layer_blocks // span, some)

    def iterate(it):
        gather_group(it)
        loop(count // batch, lambda c: send_batch(it, c * batch))
        halo[it, my_rows, :] = send[it, self_k]

        @pl.when(it == 0)
        def _():
            for copy in inputs[8:10]:
                copy.wait()

        total[...] = jnp.dot(
            tile_rows(0, group_blocks, 0, group_blocks), table[it, core], preferred_element_type=F32
        )
        arrived = lambda k: swap_copy(it, k).wait_recv()
        loop(self_k, arrived)
        layer(it, low)
        layer(it, lax.rem(low + 2, Z_LO))
        loop(count, arrived, self_k + 1)
        layer(it, lax.rem(low + 1, Z_LO))
        layer(it, lax.rem(low + 3, Z_LO))
        adj_ref[...] = grad_ref[...] + GAMMA * total[...]

        @pl.when(it < ITERS - 1)
        def _():
            make_message(it + 1, adj_ref[...])

    loop(ITERS, iterate)

    inputs[10].wait()
    gradient = lax.dot_general(
        act_ref[...], adj_ref[...].astype(BF16), (((0,), (0,)), ((), ())), preferred_element_type=F32
    )
    piece_rows = hidden // chips
    for j in range(chips):
        part[j] = gradient[j * piece_rows : (j + 1) * piece_rows]

    def share(src, dst, sems, k, where):
        return pltpu.make_async_remote_copy(
            src_ref=src, dst_ref=dst, send_sem=sems[0].at[k], recv_sem=sems[1].at[k], device_id=where, device_id_type=MESH
        )

    def chip_ahead(k):
        return lax.rem(chip + k, chips)

    def plane_copy(k):
        where = device(z, chip_ahead(k) * CORES + core)
        return share(part.at[chip_ahead(k)], plane_sum.at[chip], (plane_send, plane_recv), k, where)

    loop(chips, lambda k: plane_copy(k).start(), 1)
    plane_sum[chip] = part[chip]
    loop(chips, lambda k: plane_copy(k).wait(), 1)

    mine = m * CORES + core
    near_sum[mine] = jnp.sum(plane_sum[...], axis=0)

    def near_copies():
        for k in range(CORES * narrow):
            if k > 0:
                where = device(lax.rem(z + Z_LO * (k // CORES), depth), twin if k % CORES else me)
                yield share(near_sum.at[mine], near_sum.at[mine], (near_send, near_recv), k, where)

    for copy in near_copies():
        copy.start()
    for copy in near_copies():
        copy.wait()

    low_sum[low] = jnp.sum(near_sum[...], axis=0)

    def low_copies():
        for k, step in enumerate((1, depth - 1, jnp.where(even, 2, depth - 2))):
            where = device(lax.rem(z + step, depth), me)
            yield share(low_sum.at[low], low_sum.at[low], (low_send, low_recv), k, where)

    for copy in low_copies():
        copy.start()
    for copy in low_copies():
        copy.wait()
    wg_all[chip] = jnp.sum(low_sum[...], axis=0) * scale

    def last_copy(k):
        where = device(z, chip_ahead(k) * CORES + core)
        return share(wg_all.at[chip], wg_all.at[chip], (last_send, last_recv), k, where)

    loop(chips, lambda k: last_copy(k).start(), 1)
    loop(chips, lambda k: last_copy(k).wait(), 1)
    wg_ref[...] = wg_all[...]

    def sent(it):
        for k in range(1, narrow):
            group_copy(it, k).wait_send()
        for k in range(narrow):
            twin_copy(it, k).wait_send()
        partners(lambda k: swap_copy(it, k).wait_send())

    loop(ITERS, sent)


def per_device(
    grad_in,
    phi_slope,
    activations,
    weight,
    local_tiles,
    local_rows,
    local_cols,
    local_count,
    remote_tiles,
    remote_rows,
    remote_cols,
    remote_count,
    send_list,
):
    wide, narrow = lax.axis_size("wide"), lax.axis_size("narrow")
    plane = wide // Z_LO
    chips = plane // CORES
    rows, hidden = grad_in.shape
    tb = local_tiles.shape[2]
    sendn = send_list.shape[2]
    n_local, n_remote = local_tiles.shape[1], remote_tiles.shape[1]
    count = Z_LO * chips
    batch = math.gcd(count // 2, 8)
    scale = GAMMA / math.sqrt(rows * wide * narrow)
    vmem = pl.BlockSpec(memory_space=pltpu.VMEM)
    hbm = pl.BlockSpec(memory_space=pltpu.HBM)
    smem = pl.BlockSpec(memory_space=pltpu.SMEM)
    piece = (hidden // chips, hidden)
    dma = pltpu.SemaphoreType.DMA
    pair = lambda *shape: [dma(shape), dma(shape)]
    adjoint, weight_grad = pl.pallas_call(
        functools.partial(kernel, (plane, narrow, rows, tb, sendn, batch, scale)),
        out_shape=(
            jax.ShapeDtypeStruct((rows, hidden), F32),
            jax.ShapeDtypeStruct((chips,) + piece, F32),
        ),
        in_specs=[smem] * 2 + [hbm] * 11,
        out_specs=(vmem, vmem),
        scratch_shapes=[
            pltpu.VMEM((rows, hidden), F32),
            pltpu.VMEM((rows, hidden), BF16),
            pltpu.VMEM((rows, hidden), BF16),
            pltpu.VMEM((hidden, hidden), BF16),
            pltpu.VMEM((wide, sendn), jnp.int32),
            pltpu.VMEM((n_local + n_remote + 1, tb, tb), BF16),
            pltpu.VMEM((2, n_local), jnp.int32),
            pltpu.VMEM((2, n_remote), jnp.int32),
            pltpu.VMEM((8, 128), jnp.int32),
            pltpu.SMEM((8, 128), jnp.int32),
            pltpu.VMEM((ITERS, CORES, narrow * rows, hidden), BF16),
            pltpu.VMEM((CORES, wide, sendn), jnp.int32),
            pltpu.VMEM((count, CORES * sendn, 128), jnp.int32),
            pltpu.VMEM((ITERS, count, CORES * sendn, hidden), BF16),
            pltpu.VMEM((ITERS, wide * sendn, hidden), BF16),
            pltpu.VMEM((rows, hidden), F32),
            pltpu.VMEM((chips,) + piece, F32),
            pltpu.VMEM((chips,) + piece, F32),
            pltpu.VMEM((CORES * narrow,) + piece, F32),
            pltpu.VMEM((Z_LO,) + piece, F32),
            pltpu.VMEM((chips,) + piece, F32),
            dma((11,)),
            dma,
        ]
        + pair(3)
        + pair(ITERS, narrow)
        + pair(ITERS, narrow)
        + pair(ITERS, count)
        + pair(chips)
        + pair(CORES * narrow)
        + pair(3)
        + pair(chips),
        compiler_params=pltpu.CompilerParams(
            collective_id=0, has_side_effects=True, vmem_limit_bytes=61 * 1024 * 1024
        ),
    )(
        local_count,
        remote_count,
        grad_in,
        phi_slope,
        activations,
        weight,
        send_list[0],
        local_tiles[0],
        remote_tiles[0],
        local_rows,
        local_cols,
        remote_rows,
        remote_cols,
    )
    return adjoint, weight_grad.reshape(hidden, hidden)


def solution(mesh):
    placed = (
        P(("wide", "narrow"), None),
        P(("wide", "narrow"), None),
        P(("wide", "narrow"), None),
        P(),
        P(("wide", "narrow"), None, None, None),
        P(("wide", "narrow"), None),
        P(("wide", "narrow"), None),
        P(("wide", "narrow")),
        P(("wide", "narrow"), None, None, None),
        P(("wide", "narrow"), None),
        P(("wide", "narrow"), None),
        P(("wide", "narrow")),
        P(("wide", "narrow"), None, None),
    )
    return jax.shard_map(
        per_device,
        mesh=mesh,
        in_specs=placed,
        out_specs=(P(("wide", "narrow"), None), P()),
        check_vma=False,
    )
```

```python
import functools
import math

import jax
import jax.numpy as jnp
from jax import lax
from jax.experimental import pallas as pl
from jax.experimental.pallas import tpu as pltpu
from jax.sharding import PartitionSpec as P

ITERS = 2
GAMMA = 0.5
Z_LO = 4
CORES = 2
MESH = pl.DeviceIdType.MESH
F32 = jnp.float32
BF16 = jnp.bfloat16


def loop(count, body, start=0):
    def step(i, carry):
        body(i)
        return carry

    lax.fori_loop(start, count, step, 0)


def kernel(
    cfg,
    local_count,
    remote_count,
    grad_hbm,
    phi_hbm,
    act_hbm,
    weight_hbm,
    list_hbm,
    local_hbm,
    remote_hbm,
    local_rows,
    local_cols,
    remote_rows,
    remote_cols,
    adj_hbm,
    wg_ref,
    adj_ref,
    grad_ref,
    phi_ref,
    act_ref,
    weight_ref,
    list_ref,
    tiles,
    local_at,
    remote_at,
    slot_rows,
    slot_of,
    table,
    lists,
    index,
    picked,
    send,
    halo,
    total,
    part,
    plane_sum,
    column_sum,
    wg_all,
    know_plane,
    know_space,
    in_sem,
    slot_sem,
    out_sem,
    list_send,
    list_recv,
    group_send,
    group_recv,
    twin_send,
    twin_recv,
    swap_send,
    swap_recv,
    plane_send,
    plane_recv,
    column_send,
    column_recv,
    last_send,
    last_recv,
):
    plane, narrow, rows, tb, sendn, batch, scale = cfg
    depth = Z_LO * narrow
    chips = plane // CORES
    side = math.isqrt(chips)
    count = Z_LO * chips
    per_chip = CORES * sendn
    hidden = grad_ref.shape[1]
    n_local, n_remote = local_hbm.shape[0], remote_hbm.shape[0]
    zero_slot = n_local + n_remote
    blocks = rows // tb
    group_rows = narrow * rows
    group_blocks = narrow * blocks
    layer_blocks = chips * per_chip // tb
    halo_blocks = Z_LO * layer_blocks
    span = math.gcd(layer_blocks, 7)

    wide_at, m = lax.axis_index("wide"), lax.axis_index("narrow")
    low, me = wide_at // plane, lax.rem(wide_at, plane)
    z = m * Z_LO + low
    core, chip = lax.rem(me, CORES), me // CORES
    twin = me + 1 - 2 * core
    even = lax.rem(low, 2) == 0

    def device(z_at, in_plane):
        return (lax.rem(z_at, Z_LO) * plane + in_plane, z_at // Z_LO)

    def offset(k):
        phase, inner = k // (count // 2), lax.rem(k, count // 2)
        turn, j = lax.rem(inner, 2), inner // 2
        i_x = j // side
        i_y = lax.rem(j, side)

        def far_first(i):
            if side == 1:
                return 0 * i
            return jnp.where(i == 0, 2, jnp.where(i == 1, 1, jnp.where(i == 2, 3, 0)))

        dx, dy = far_first(i_x), far_first(i_y)
        dx = jnp.where(turn == 0, dx, lax.rem(side - dx, side))
        dy = jnp.where(turn == 0, dy, lax.rem(side - dy, side))
        two = jnp.where(even, 2, depth - 2)
        dz = jnp.where(phase == 0, jnp.where(turn == 0, two, 0), jnp.where(turn == 0, 1, depth - 1))
        return dz, dx, dy

    self_k = count // 2 - 1

    def target(k):
        dz, dx, dy = offset(k)
        return lax.rem(z + dz, depth), lax.rem(chip // side + dx, side) * side + lax.rem(lax.rem(chip, side) + dy, side)

    def partners(body):
        loop(self_k, body)
        loop(count, body, self_k + 1)

    barrier = pltpu.get_barrier_semaphore()

    def greet(where):
        pl.semaphore_signal(barrier, inc=1, device_id=where, device_id_type=MESH)

    x, y = chip // side, lax.rem(chip, side)
    x_line = [device(z, (lax.rem(x + k, side) * side + y) * CORES + core) for k in range(1, side)]
    y_line = [device(z, (x * side + lax.rem(y + k, side)) * CORES + core) for k in range(1, side)]
    z_line = [device(lax.rem(z + k, depth), me) for k in (1, 2, depth - 2, depth - 1)]
    group = [device(lax.rem(z + Z_LO * k, depth), me) for k in range(1, narrow)]
    first_round = z_line + group + x_line + y_line + [device(z, twin)]
    for where in first_round:
        greet(where)

    def tell(semaphore, listeners):
        for where in listeners:
            pl.semaphore_signal(semaphore, inc=1, device_id=where, device_id_type=MESH)
        if listeners:
            pl.semaphore_wait(semaphore, len(listeners))

    inputs = [
        (grad_hbm, grad_ref),
        (phi_hbm, phi_ref),
        (weight_hbm, weight_ref),
        (list_hbm, list_ref),
        (local_rows, local_at.at[0:1]),
        (local_cols, local_at.at[1:2]),
        (remote_rows, remote_at.at[0:1]),
        (remote_cols, remote_at.at[1:2]),
        (local_hbm, tiles.at[pl.ds(0, n_local)]),
        (remote_hbm, tiles.at[pl.ds(n_local, n_remote)]),
        (act_hbm, act_ref),
    ]
    inputs = [pltpu.make_async_copy(src, dst, in_sem.at[i]) for i, (src, dst) in enumerate(inputs)]
    for copy in inputs:
        copy.start()

    def make_message(it, adjoint):
        mapped = lax.dot_general(
            adjoint.astype(BF16), weight_ref[...], (((1,), (1,)), ((), ())), preferred_element_type=F32
        )
        message = (mapped * phi_ref[...].astype(F32)).astype(BF16)
        table[it, core, pl.ds(pl.multiple_of(m * rows, rows), rows), :] = message

    for copy in inputs[:3]:
        copy.wait()
    make_message(0, grad_ref[...])
    pl.semaphore_wait(barrier, len(first_round))

    def group_block(it, g, k):
        at = pl.multiple_of(lax.rem(m + narrow - k, narrow) * rows, rows)
        return table.at[it, g, pl.ds(at, rows)]

    def group_copy(it, k):
        return pltpu.make_async_remote_copy(
            src_ref=group_block(it, core, 0),
            dst_ref=group_block(it, core, 0),
            send_sem=group_send.at[it, k],
            recv_sem=group_recv.at[it, k],
            device_id=device(lax.rem(z + Z_LO * k, depth), me),
            device_id_type=MESH,
        )

    def twin_copy(it, k):
        return pltpu.make_async_remote_copy(
            src_ref=group_block(it, core, k),
            dst_ref=group_block(it, core, k),
            send_sem=twin_send.at[it, k],
            recv_sem=twin_recv.at[it, k],
            device_id=device(z, twin),
            device_id_type=MESH,
        )

    away = jnp.where(low < Z_LO // 2, Z_LO - 1, 0)
    holder = lax.rem(z + jnp.where(low < Z_LO // 2, Z_LO, depth - Z_LO), depth)

    def list_copy(i):
        src, kind, where = (
            (list_ref, 1, device(holder, me)),
            (list_ref, 0, device(z, twin)),
            (lists.at[1, core], 1, device(z, twin)),
        )[i]
        return pltpu.make_async_remote_copy(
            src_ref=src,
            dst_ref=lists.at[kind, core],
            send_sem=list_send.at[i],
            recv_sem=list_recv.at[i],
            device_id=where,
            device_id_type=MESH,
        )

    def make_index(g):
        lane = lax.broadcasted_iota(jnp.int32, (sendn, Z_LO * plane), 1)
        is_away = (lane >= away * plane) & (lane < (away + 1) * plane)
        merged = jnp.where(is_away, lists[1, g], lists[0, g])
        merged = jnp.where(core == 0, merged, pltpu.roll(merged, Z_LO * plane - 1, 1))
        for c in range(count):
            at = c * CORES
            index[c, g * sendn : (g + 1) * sendn, :] = jnp.broadcast_to(merged[:, at : at + 1], (sendn, 128))

    def make_slots():
        def row_of(at, alive, per_row, first):
            key = at[0:1] * per_row + at[1:2]
            slot = lax.broadcasted_iota(jnp.int32, key.shape, 1)
            key = jnp.where(slot < alive, key, -1)
            wide_key = jnp.broadcast_to(key, (128, key.shape[1]))
            pair = lax.broadcasted_iota(jnp.int32, wide_key.shape, 0)
            value = lax.broadcasted_iota(jnp.int32, wide_key.shape, 1) + (first - zero_slot)
            found = zero_slot + jnp.sum(jnp.where(wide_key == pair, value, 0), axis=1, keepdims=True)
            return jnp.transpose(jnp.broadcast_to(found, (128, 128)))[0:1]

        slot_rows[0:1] = row_of(local_at[...], local_count[0], group_blocks, 0)
        slot_rows[1:2] = row_of(remote_at[...], remote_count[0], halo_blocks, n_local)
        copy = pltpu.make_async_copy(slot_rows, slot_of, slot_sem)
        copy.start()
        copy.wait()

    my_rows = pl.ds(pl.multiple_of((low * chips + chip) * per_chip, 16), per_chip)

    def swap_copy(it, k):
        z_at, chip_at = target(k)
        return pltpu.make_async_remote_copy(
            src_ref=send.at[it, k],
            dst_ref=halo.at[it, my_rows],
            send_sem=swap_send.at[it, k],
            recv_sem=swap_recv.at[it, k],
            device_id=device(z_at, chip_at * CORES + core),
            device_id_type=MESH,
        )

    batches = count // batch
    early = batches // 2

    def select(it, c, g):
        wanted = []
        for j in range(batch):
            z_at, chip_at = target(c * batch + j)
            wanted.append(lax.rem(z_at, Z_LO) * chips + chip_at)
        g_rows = pl.ds(pl.multiple_of(g * sendn, 8), sendn)
        want = jnp.concatenate([index[w, g_rows, :] for w in wanted], axis=0)
        lane = lax.broadcasted_iota(jnp.int32, want.shape, 1)
        hot = jnp.concatenate(
            [jnp.where(want == lane + at, 1.0, 0.0).astype(BF16) for at in range(0, group_rows, 128)], axis=1
        )
        got = jnp.dot(hot, table[it, g], preferred_element_type=F32)
        for j in range(batch):
            picked[c, j, g_rows, :] = got[j * sendn : (j + 1) * sendn]

    def send_batch(it, c):
        def post(j):
            k = c * batch + j
            send[it, k] = picked[c, j].astype(BF16)

            @pl.when(k != self_k)
            def _():
                swap_copy(it, k).start()

        select(it, c, 1 - core)
        loop(batch, post)

    def both_then_send(it, c):
        select(it, c, core)
        send_batch(it, c)

    def tile_rows(kind, per_row, first, width):
        return jnp.concatenate(
            [
                jnp.concatenate([tiles[slot_of[kind, r * per_row + first + c]] for c in range(width)], axis=1)
                for r in range(blocks)
            ],
            axis=0,
        )

    def gather_group(it):
        far_first = sorted(range(1, narrow), key=lambda k: -min(k, narrow - k))
        for k in far_first:
            group_copy(it, k).start()
        twin_copy(it, 0).start()

        @pl.when(it == 0)
        def _():
            inputs[3].wait()
            list_copy(0).start()
            list_copy(1).start()
            lists[0, core] = list_ref[...]
            tell(know_plane, x_line)
            tell(know_space, z_line + [device(z, twin)])
            for copy in inputs[4:8]:
                copy.wait()
            tiles[zero_slot] = jnp.zeros((tb, tb), BF16)
            make_slots()

        for i, k in enumerate(reversed(far_first)):
            group_copy(it, k).wait_recv()
            twin_copy(it, k).start()
            if i == 0:

                @pl.when(it == 0)
                def _():
                    list_copy(0).wait_recv()
                    list_copy(2).start()
                    list_copy(1).wait_recv()
                    list_copy(2).wait_recv()
                    for g in range(CORES):
                        make_index(g)
                    for i in range(3):
                        list_copy(i).wait_send()
                    for copy in inputs[8:10]:
                        copy.wait()

        loop(early, lambda c: select(it, c, core))
        total[...] = jnp.dot(
            tile_rows(0, group_blocks, 0, group_blocks), table[it, core], preferred_element_type=F32
        )
        for k in range(narrow):
            twin_copy(it, k).wait_recv()

    def layer(it, b):
        def some(i):
            first = b * layer_blocks + i * span
            source = halo[it, pl.ds(pl.multiple_of(first * tb, tb), span * tb), :]
            total[...] += jnp.dot(tile_rows(1, halo_blocks, first, span), source, preferred_element_type=F32)

        loop(layer_blocks // span, some)

    def iterate(it):
        gather_group(it)
        loop(early, lambda c: send_batch(it, c))
        loop(batches, lambda c: both_then_send(it, c), early)
        halo[it, my_rows, :] = send[it, self_k]
        arrived = lambda k: swap_copy(it, k).wait_recv()
        loop(self_k, arrived)
        layer(it, low)
        layer(it, lax.rem(low + 2, Z_LO))
        loop(count, arrived, self_k + 1)
        layer(it, lax.rem(low + 1, Z_LO))
        layer(it, lax.rem(low + 3, Z_LO))
        adj_ref[...] = grad_ref[...] + GAMMA * total[...]

        @pl.when(it < ITERS - 1)
        def _():
            make_message(it + 1, adj_ref[...])

    loop(ITERS, iterate)
    adj_copy = pltpu.make_async_copy(adj_ref, adj_hbm, out_sem)
    adj_copy.start()

    inputs[10].wait()
    gradient = lax.dot_general(
        act_ref[...], adj_ref[...].astype(BF16), (((0,), (0,)), ((), ())), preferred_element_type=F32
    )
    piece_rows = hidden // chips
    for j in range(chips):
        part[j] = gradient[j * piece_rows : (j + 1) * piece_rows]

    def share(src, dst, sems, k, where):
        return pltpu.make_async_remote_copy(
            src_ref=src, dst_ref=dst, send_sem=sems[0].at[k], recv_sem=sems[1].at[k], device_id=where, device_id_type=MESH
        )

    def chip_ahead(k):
        return lax.rem(chip + k, chips)

    def plane_copy(k):
        other = lax.rem(me + k, plane)
        return share(part.at[other // CORES], plane_sum.at[me], (plane_send, plane_recv), k, device(z, other))

    loop(plane, lambda k: plane_copy(k).start(), 1)
    plane_sum[me] = part[chip]
    loop(plane, lambda k: plane_copy(k).wait_recv(), 1)
    column_sum[z] = jnp.sum(plane_sum[...], axis=0)

    def column_copy(k):
        where = device(lax.rem(z + k, depth), me)
        return share(column_sum.at[z], column_sum.at[z], (column_send, column_recv), k, where)

    for k in sorted(range(1, depth), key=lambda k: -min(k, depth - k)):
        column_copy(k).start()
    loop(depth, lambda k: column_copy(k).wait_recv(), 1)
    wg_all[chip] = jnp.sum(column_sum[...], axis=0) * scale

    def last_copy(k):
        where = device(z, chip_ahead(k) * CORES + core)
        return share(wg_all.at[chip], wg_all.at[chip], (last_send, last_recv), k, where)

    loop(chips, lambda k: last_copy(k).start(), 1)
    loop(chips, lambda k: last_copy(k).wait_recv(), 1)
    wg_ref[...] = wg_all[...]
    loop(plane, lambda k: plane_copy(k).wait_send(), 1)
    loop(depth, lambda k: column_copy(k).wait_send(), 1)
    loop(chips, lambda k: last_copy(k).wait_send(), 1)
    adj_copy.wait()

    def sent(it):
        for k in range(1, narrow):
            group_copy(it, k).wait_send()
        for k in range(narrow):
            twin_copy(it, k).wait_send()
        partners(lambda k: swap_copy(it, k).wait_send())

    loop(ITERS, sent)


def per_device(
    grad_in,
    phi_slope,
    activations,
    weight,
    local_tiles,
    local_rows,
    local_cols,
    local_count,
    remote_tiles,
    remote_rows,
    remote_cols,
    remote_count,
    send_list,
):
    wide, narrow = lax.axis_size("wide"), lax.axis_size("narrow")
    plane = wide // Z_LO
    chips = plane // CORES
    rows, hidden = grad_in.shape
    tb = local_tiles.shape[2]
    sendn = send_list.shape[2]
    n_local, n_remote = local_tiles.shape[1], remote_tiles.shape[1]
    count = Z_LO * chips
    batch = math.gcd(count // 2, 8)
    scale = GAMMA / math.sqrt(rows * wide * narrow)
    vmem = pl.BlockSpec(memory_space=pltpu.VMEM)
    hbm = pl.BlockSpec(memory_space=pltpu.HBM)
    smem = pl.BlockSpec(memory_space=pltpu.SMEM)
    piece = (hidden // chips, hidden)
    dma = pltpu.SemaphoreType.DMA
    pair = lambda *shape: [dma(shape), dma(shape)]
    adjoint, weight_grad = pl.pallas_call(
        functools.partial(kernel, (plane, narrow, rows, tb, sendn, batch, scale)),
        out_shape=(
            jax.ShapeDtypeStruct((rows, hidden), F32),
            jax.ShapeDtypeStruct((chips,) + piece, F32),
        ),
        in_specs=[smem] * 2 + [hbm] * 11,
        out_specs=(hbm, vmem),
        scratch_shapes=[
            pltpu.VMEM((rows, hidden), F32),
            pltpu.VMEM((rows, hidden), F32),
            pltpu.VMEM((rows, hidden), BF16),
            pltpu.VMEM((rows, hidden), BF16),
            pltpu.VMEM((hidden, hidden), BF16),
            pltpu.VMEM((sendn, wide), jnp.int32),
            pltpu.VMEM((n_local + n_remote + 1, tb, tb), BF16),
            pltpu.VMEM((2, n_local), jnp.int32),
            pltpu.VMEM((2, n_remote), jnp.int32),
            pltpu.VMEM((8, 128), jnp.int32),
            pltpu.SMEM((8, 128), jnp.int32),
            pltpu.VMEM((ITERS, CORES, narrow * rows, hidden), BF16),
            pltpu.VMEM((2, CORES, sendn, wide), jnp.int32),
            pltpu.VMEM((count, CORES * sendn, 128), jnp.int32),
            pltpu.VMEM((count // batch, batch, CORES * sendn, hidden), F32),
            pltpu.VMEM((ITERS, count, CORES * sendn, hidden), BF16),
            pltpu.VMEM((ITERS, wide * sendn, hidden), BF16),
            pltpu.VMEM((rows, hidden), F32),
            pltpu.VMEM((chips,) + piece, F32),
            pltpu.VMEM((plane,) + piece, F32),
            pltpu.VMEM((Z_LO * narrow,) + piece, F32),
            pltpu.VMEM((chips,) + piece, F32),
            pltpu.SemaphoreType.REGULAR,
            pltpu.SemaphoreType.REGULAR,
            dma((11,)),
            dma,
            dma,
        ]
        + pair(3)
        + pair(ITERS, narrow)
        + pair(ITERS, narrow)
        + pair(ITERS, count)
        + pair(plane)
        + pair(Z_LO * narrow)
        + pair(chips),
        compiler_params=pltpu.CompilerParams(
            collective_id=0, has_side_effects=True, vmem_limit_bytes=61 * 1024 * 1024
        ),
    )(
        local_count,
        remote_count,
        grad_in,
        phi_slope,
        activations,
        weight,
        jnp.transpose(send_list[0]),
        local_tiles[0],
        remote_tiles[0],
        local_rows,
        local_cols,
        remote_rows,
        remote_cols,
    )
    return adjoint, weight_grad.reshape(hidden, hidden)


def solution(mesh):
    placed = (
        P(("wide", "narrow"), None),
        P(("wide", "narrow"), None),
        P(("wide", "narrow"), None),
        P(),
        P(("wide", "narrow"), None, None, None),
        P(("wide", "narrow"), None),
        P(("wide", "narrow"), None),
        P(("wide", "narrow")),
        P(("wide", "narrow"), None, None, None),
        P(("wide", "narrow"), None),
        P(("wide", "narrow"), None),
        P(("wide", "narrow")),
        P(("wide", "narrow"), None, None),
    )
    return jax.shard_map(
        per_device,
        mesh=mesh,
        in_specs=placed,
        out_specs=(P(("wide", "narrow"), None), P()),
        check_vma=False,
    )
```

```python
import functools
import math

import jax
import jax.numpy as jnp
from jax import lax
from jax.experimental import pallas as pl
from jax.experimental.pallas import tpu as pltpu
from jax.sharding import PartitionSpec as P

ITERS = 2
GAMMA = 0.5
Z_LO = 4
CORES = 2
MESH = pl.DeviceIdType.MESH
F32 = jnp.float32
BF16 = jnp.bfloat16


def loop(count, body, start=0):
    def step(i, carry):
        body(i)
        return carry

    lax.fori_loop(start, count, step, 0)


def kernel(
    cfg,
    local_count,
    remote_count,
    grad_hbm,
    phi_hbm,
    act_hbm,
    weight_hbm,
    list_hbm,
    local_hbm,
    remote_hbm,
    local_rows,
    local_cols,
    remote_rows,
    remote_cols,
    adj_hbm,
    wg_ref,
    adj_ref,
    grad_ref,
    phi_ref,
    act_ref,
    weight_ref,
    list_ref,
    tiles,
    local_at,
    remote_at,
    slot_rows,
    slot_of,
    table,
    lists,
    index,
    picked,
    send,
    halo,
    total,
    part,
    plane_sum,
    column_sum,
    wg_all,
    know_plane,
    know_space,
    in_sem,
    slot_sem,
    out_sem,
    list_send,
    list_recv,
    group_send,
    group_recv,
    twin_send,
    twin_recv,
    swap_send,
    swap_recv,
    plane_send,
    plane_recv,
    column_send,
    column_recv,
    last_send,
    last_recv,
):
    plane, narrow, rows, tb, sendn, batch, scale = cfg
    depth = Z_LO * narrow
    chips = plane // CORES
    side = math.isqrt(chips)
    count = Z_LO * chips
    per_chip = CORES * sendn
    hidden = grad_ref.shape[1]
    n_local, n_remote = local_hbm.shape[0], remote_hbm.shape[0]
    zero_slot = n_local + n_remote
    blocks = rows // tb
    group_rows = narrow * rows
    group_blocks = narrow * blocks
    layer_blocks = chips * per_chip // tb
    halo_blocks = Z_LO * layer_blocks
    span = math.gcd(layer_blocks, 7)

    wide_at, m = lax.axis_index("wide"), lax.axis_index("narrow")
    low, me = wide_at // plane, lax.rem(wide_at, plane)
    z = m * Z_LO + low
    core, chip = lax.rem(me, CORES), me // CORES
    twin = me + 1 - 2 * core
    even = lax.rem(low, 2) == 0

    def device(z_at, in_plane):
        return (lax.rem(z_at, Z_LO) * plane + in_plane, z_at // Z_LO)

    def offset(k):
        phase, inner = k // (count // 2), lax.rem(k, count // 2)
        turn, j = lax.rem(inner, 2), inner // 2
        i_x = j // side
        i_y = lax.rem(j, side)

        def far_first(i):
            if side == 1:
                return 0 * i
            return jnp.where(i == 0, 2, jnp.where(i == 1, 1, jnp.where(i == 2, 3, 0)))

        dx, dy = far_first(i_x), far_first(i_y)
        dx, dy = jnp.where(core == 0, dx, dy), jnp.where(core == 0, dy, dx)
        dx = jnp.where(turn == 0, dx, lax.rem(side - dx, side))
        dy = jnp.where(turn == 0, dy, lax.rem(side - dy, side))
        two = jnp.where(even, 2, depth - 2)
        dz = jnp.where(phase == 0, jnp.where(turn == 0, two, 0), jnp.where(turn == 0, 1, depth - 1))
        return dz, dx, dy

    self_k = count // 2 - 1

    def target(k):
        dz, dx, dy = offset(k)
        return lax.rem(z + dz, depth), lax.rem(chip // side + dx, side) * side + lax.rem(lax.rem(chip, side) + dy, side)

    def partners(body):
        loop(self_k, body)
        loop(count, body, self_k + 1)

    barrier = pltpu.get_barrier_semaphore()

    def greet(where):
        pl.semaphore_signal(barrier, inc=1, device_id=where, device_id_type=MESH)

    x, y = chip // side, lax.rem(chip, side)
    x_line = [device(z, (lax.rem(x + k, side) * side + y) * CORES + core) for k in range(1, side)]
    y_line = [device(z, (x * side + lax.rem(y + k, side)) * CORES + core) for k in range(1, side)]
    z_line = [device(lax.rem(z + k, depth), me) for k in (1, 2, depth - 2, depth - 1)]
    group = [device(lax.rem(z + Z_LO * k, depth), me) for k in range(1, narrow)]
    first_round = z_line + group + x_line + y_line + [device(z, twin)]
    for where in first_round:
        greet(where)

    def tell(semaphore, listeners):
        for where in listeners:
            pl.semaphore_signal(semaphore, inc=1, device_id=where, device_id_type=MESH)
        if listeners:
            pl.semaphore_wait(semaphore, len(listeners))

    inputs = [
        (grad_hbm, grad_ref),
        (phi_hbm, phi_ref),
        (weight_hbm, weight_ref),
        (list_hbm, list_ref),
        (local_rows, local_at.at[0:1]),
        (local_cols, local_at.at[1:2]),
        (remote_rows, remote_at.at[0:1]),
        (remote_cols, remote_at.at[1:2]),
        (local_hbm, tiles.at[pl.ds(0, n_local)]),
        (remote_hbm, tiles.at[pl.ds(n_local, n_remote)]),
        (act_hbm, act_ref),
    ]
    inputs = [pltpu.make_async_copy(src, dst, in_sem.at[i]) for i, (src, dst) in enumerate(inputs)]
    for copy in inputs:
        copy.start()

    def make_message(it, adjoint):
        mapped = lax.dot_general(
            adjoint.astype(BF16), weight_ref[...], (((1,), (1,)), ((), ())), preferred_element_type=F32
        )
        message = (mapped * phi_ref[...].astype(F32)).astype(BF16)
        table[it, core, pl.ds(pl.multiple_of(m * rows, rows), rows), :] = message

    for copy in inputs[:3]:
        copy.wait()
    make_message(0, grad_ref[...])
    pl.semaphore_wait(barrier, len(first_round))

    half = rows // 2

    def group_half(it, k, piece):
        at = pl.multiple_of(lax.rem(m + narrow - k, narrow) * rows + piece * half, half)
        return table.at[it, core, pl.ds(at, half)]

    hops = ((1, 0, 0), (-1, 0, 1), (1, 0, 1), (-1, 0, 0), (1, 1, 0), (-1, narrow - 1, 1))

    def group_copy(it, i):
        way, k, piece = hops[i]
        ref = group_half(it, k, piece)
        return pltpu.make_async_remote_copy(
            src_ref=ref,
            dst_ref=ref,
            send_sem=group_send.at[it, i],
            recv_sem=group_recv.at[it, i],
            device_id=device(lax.rem(z + depth + way * Z_LO, depth), me),
            device_id_type=MESH,
        )

    def twin_copy(it, k, piece):
        ref = group_half(it, k, piece)
        return pltpu.make_async_remote_copy(
            src_ref=ref,
            dst_ref=ref,
            send_sem=twin_send.at[it, CORES * k + piece],
            recv_sem=twin_recv.at[it, CORES * k + piece],
            device_id=device(z, twin),
            device_id_type=MESH,
        )

    away = jnp.where(low < Z_LO // 2, Z_LO - 1, 0)
    holder = lax.rem(z + jnp.where(low < Z_LO // 2, Z_LO, depth - Z_LO), depth)

    def list_copy(i):
        src, kind, where = (
            (list_ref, 1, device(holder, me)),
            (list_ref, 0, device(z, twin)),
            (lists.at[1, core], 1, device(z, twin)),
        )[i]
        return pltpu.make_async_remote_copy(
            src_ref=src,
            dst_ref=lists.at[kind, core],
            send_sem=list_send.at[i],
            recv_sem=list_recv.at[i],
            device_id=where,
            device_id_type=MESH,
        )

    def make_index(g):
        lane = lax.broadcasted_iota(jnp.int32, (sendn, Z_LO * plane), 1)
        is_away = (lane >= away * plane) & (lane < (away + 1) * plane)
        merged = jnp.where(is_away, lists[1, g], lists[0, g])
        merged = jnp.where(core == 0, merged, pltpu.roll(merged, Z_LO * plane - 1, 1))
        for c in range(count):
            at = c * CORES
            index[c, g * sendn : (g + 1) * sendn, :] = jnp.broadcast_to(merged[:, at : at + 1], (sendn, 128))

    def make_slots():
        def row_of(at, alive, per_row, first):
            key = at[0:1] * per_row + at[1:2]
            slot = lax.broadcasted_iota(jnp.int32, key.shape, 1)
            key = jnp.where(slot < alive, key, -1)
            wide_key = jnp.broadcast_to(key, (128, key.shape[1]))
            pair = lax.broadcasted_iota(jnp.int32, wide_key.shape, 0)
            value = lax.broadcasted_iota(jnp.int32, wide_key.shape, 1) + (first - zero_slot)
            found = zero_slot + jnp.sum(jnp.where(wide_key == pair, value, 0), axis=1, keepdims=True)
            return jnp.transpose(jnp.broadcast_to(found, (128, 128)))[0:1]

        slot_rows[0:1] = row_of(local_at[...], local_count[0], group_blocks, 0)
        slot_rows[1:2] = row_of(remote_at[...], remote_count[0], halo_blocks, n_local)
        copy = pltpu.make_async_copy(slot_rows, slot_of, slot_sem)
        copy.start()
        copy.wait()

    my_rows = pl.ds(pl.multiple_of((low * chips + chip) * per_chip, 16), per_chip)

    def swap_copy(it, k):
        z_at, chip_at = target(k)
        return pltpu.make_async_remote_copy(
            src_ref=send.at[it, k],
            dst_ref=halo.at[it, my_rows],
            send_sem=swap_send.at[it, k],
            recv_sem=swap_recv.at[it, k],
            device_id=device(z_at, chip_at * CORES + core),
            device_id_type=MESH,
        )

    batches = count // batch
    early = batches // 2

    def select(it, c, g):
        wanted = []
        for j in range(batch):
            z_at, chip_at = target(c * batch + j)
            wanted.append(lax.rem(z_at, Z_LO) * chips + chip_at)
        g_rows = pl.ds(pl.multiple_of(g * sendn, 8), sendn)
        want = jnp.concatenate([index[w, g_rows, :] for w in wanted], axis=0)
        lane = lax.broadcasted_iota(jnp.int32, want.shape, 1)
        hot = jnp.concatenate(
            [jnp.where(want == lane + at, 1.0, 0.0).astype(BF16) for at in range(0, group_rows, 128)], axis=1
        )
        got = jnp.dot(hot, table[it, g], preferred_element_type=F32)
        for j in range(batch):
            picked[c, j, g_rows, :] = got[j * sendn : (j + 1) * sendn]

    def send_batch(it, c):
        def post(j):
            k = c * batch + j
            send[it, k] = picked[c, j].astype(BF16)

            @pl.when(k != self_k)
            def _():
                swap_copy(it, k).start()

        select(it, c, 1 - core)
        loop(batch, post)

    def both_then_send(it, c):
        select(it, c, core)
        send_batch(it, c)

    def tile_rows(kind, per_row, first, width):
        return jnp.concatenate(
            [
                jnp.concatenate([tiles[slot_of[kind, r * per_row + first + c]] for c in range(width)], axis=1)
                for r in range(blocks)
            ],
            axis=0,
        )

    def gather_group(it):
        for i in range(4):
            group_copy(it, i).start()
        for piece in range(2):
            twin_copy(it, 0, piece).start()

        @pl.when(it == 0)
        def _():
            inputs[3].wait()
            list_copy(0).start()
            list_copy(1).start()
            lists[0, core] = list_ref[...]
            tell(know_plane, x_line)
            tell(know_space, z_line + [device(z, twin)])

        for i in range(2):
            group_copy(it, i).wait_recv()
            group_copy(it, i + 4).start()

        @pl.when(it == 0)
        def _():
            for copy in inputs[4:8]:
                copy.wait()
            tiles[zero_slot] = jnp.zeros((tb, tb), BF16)
            make_slots()
            list_copy(0).wait_recv()
            list_copy(2).start()
            list_copy(1).wait_recv()
            list_copy(2).wait_recv()
            for g in range(CORES):
                make_index(g)
            for i in range(3):
                list_copy(i).wait_send()
            for copy in inputs[8:10]:
                copy.wait()

        for i, (way, k, piece) in enumerate(hops):
            if i > 1:
                group_copy(it, i).wait_recv()
            twin_copy(it, (k + narrow + way) % narrow, piece).start()

        loop(early, lambda c: select(it, c, core))
        total[...] = jnp.dot(
            tile_rows(0, group_blocks, 0, group_blocks), table[it, core], preferred_element_type=F32
        )
        for k in range(narrow):
            for piece in range(2):
                twin_copy(it, k, piece).wait_recv()

    def layer(it, b):
        def some(i):
            first = b * layer_blocks + i * span
            source = halo[it, pl.ds(pl.multiple_of(first * tb, tb), span * tb), :]
            total[...] += jnp.dot(tile_rows(1, halo_blocks, first, span), source, preferred_element_type=F32)

        loop(layer_blocks // span, some)

    def iterate(it):
        gather_group(it)
        loop(early, lambda c: send_batch(it, c))
        loop(batches, lambda c: both_then_send(it, c), early)
        halo[it, my_rows, :] = send[it, self_k]
        arrived = lambda k: swap_copy(it, k).wait_recv()
        loop(self_k, arrived)
        layer(it, low)
        layer(it, lax.rem(low + 2, Z_LO))
        loop(count, arrived, self_k + 1)
        layer(it, lax.rem(low + 1, Z_LO))
        layer(it, lax.rem(low + 3, Z_LO))
        adj_ref[...] = grad_ref[...] + GAMMA * total[...]

        @pl.when(it < ITERS - 1)
        def _():
            make_message(it + 1, adj_ref[...])

    loop(ITERS, iterate)
    adj_copy = pltpu.make_async_copy(adj_ref, adj_hbm, out_sem)
    adj_copy.start()

    inputs[10].wait()
    gradient = lax.dot_general(
        act_ref[...], adj_ref[...].astype(BF16), (((0,), (0,)), ((), ())), preferred_element_type=F32
    )
    piece_rows = hidden // chips
    for j in range(chips):
        part[j] = gradient[j * piece_rows : (j + 1) * piece_rows]

    def share(src, dst, sems, k, where):
        return pltpu.make_async_remote_copy(
            src_ref=src, dst_ref=dst, send_sem=sems[0].at[k], recv_sem=sems[1].at[k], device_id=where, device_id_type=MESH
        )

    def chip_ahead(k):
        return lax.rem(chip + k, chips)

    def plane_copy(k):
        other = lax.rem(me + k, plane)
        return share(part.at[other // CORES], plane_sum.at[me], (plane_send, plane_recv), k, device(z, other))

    loop(plane, lambda k: plane_copy(k).start(), 1)
    plane_sum[me] = part[chip]
    loop(plane, lambda k: plane_copy(k).wait_recv(), 1)
    column_sum[z] = jnp.sum(plane_sum[...], axis=0)

    def column_copy(k):
        where = device(lax.rem(z + k, depth), me)
        return share(column_sum.at[z], column_sum.at[z], (column_send, column_recv), k, where)

    for k in sorted(range(1, depth), key=lambda k: -min(k, depth - k)):
        column_copy(k).start()
    loop(depth, lambda k: column_copy(k).wait_recv(), 1)
    wg_all[chip] = jnp.sum(column_sum[...], axis=0) * scale

    def last_copy(k):
        where = device(z, chip_ahead(k) * CORES + core)
        return share(wg_all.at[chip], wg_all.at[chip], (last_send, last_recv), k, where)

    loop(chips, lambda k: last_copy(k).start(), 1)
    loop(chips, lambda k: last_copy(k).wait_recv(), 1)
    wg_ref[...] = wg_all[...]
    loop(plane, lambda k: plane_copy(k).wait_send(), 1)
    loop(depth, lambda k: column_copy(k).wait_send(), 1)
    loop(chips, lambda k: last_copy(k).wait_send(), 1)
    adj_copy.wait()

    def sent(it):
        for i in range(len(hops)):
            group_copy(it, i).wait_send()
        for k in range(narrow):
            for piece in range(2):
                twin_copy(it, k, piece).wait_send()
        partners(lambda k: swap_copy(it, k).wait_send())

    loop(ITERS, sent)


def hand_on(adj_src, wg_src, adj_dst, wg_dst, sems):
    copies = [
        pltpu.make_async_copy(adj_src, adj_dst, sems.at[0]),
        pltpu.make_async_copy(wg_src, wg_dst, sems.at[1]),
    ]
    for copy in copies:
        copy.start()
    for copy in copies:
        copy.wait()


def per_device(
    grad_in,
    phi_slope,
    activations,
    weight,
    local_tiles,
    local_rows,
    local_cols,
    local_count,
    remote_tiles,
    remote_rows,
    remote_cols,
    remote_count,
    send_list,
):
    wide, narrow = lax.axis_size("wide"), lax.axis_size("narrow")
    plane = wide // Z_LO
    chips = plane // CORES
    rows, hidden = grad_in.shape
    tb = local_tiles.shape[2]
    sendn = send_list.shape[2]
    n_local, n_remote = local_tiles.shape[1], remote_tiles.shape[1]
    count = Z_LO * chips
    batch = math.gcd(count // 2, 8)
    scale = GAMMA / math.sqrt(rows * wide * narrow)
    vmem = pl.BlockSpec(memory_space=pltpu.VMEM)
    hbm = pl.BlockSpec(memory_space=pltpu.HBM)
    smem = pl.BlockSpec(memory_space=pltpu.SMEM)
    piece = (hidden // chips, hidden)
    dma = pltpu.SemaphoreType.DMA
    pair = lambda *shape: [dma(shape), dma(shape)]
    adjoint, weight_grad = pl.pallas_call(
        functools.partial(kernel, (plane, narrow, rows, tb, sendn, batch, scale)),
        out_shape=(
            jax.ShapeDtypeStruct((rows, hidden), F32),
            jax.ShapeDtypeStruct((chips,) + piece, F32),
        ),
        in_specs=[smem] * 2 + [hbm] * 11,
        out_specs=(hbm, vmem),
        scratch_shapes=[
            pltpu.VMEM((rows, hidden), F32),
            pltpu.VMEM((rows, hidden), F32),
            pltpu.VMEM((rows, hidden), BF16),
            pltpu.VMEM((rows, hidden), BF16),
            pltpu.VMEM((hidden, hidden), BF16),
            pltpu.VMEM((sendn, wide), jnp.int32),
            pltpu.VMEM((n_local + n_remote + 1, tb, tb), BF16),
            pltpu.VMEM((2, n_local), jnp.int32),
            pltpu.VMEM((2, n_remote), jnp.int32),
            pltpu.VMEM((8, 128), jnp.int32),
            pltpu.SMEM((8, 128), jnp.int32),
            pltpu.VMEM((ITERS, CORES, narrow * rows, hidden), BF16),
            pltpu.VMEM((2, CORES, sendn, wide), jnp.int32),
            pltpu.VMEM((count, CORES * sendn, 128), jnp.int32),
            pltpu.VMEM((count // batch, batch, CORES * sendn, hidden), F32),
            pltpu.VMEM((ITERS, count, CORES * sendn, hidden), BF16),
            pltpu.VMEM((ITERS, wide * sendn, hidden), BF16),
            pltpu.VMEM((rows, hidden), F32),
            pltpu.VMEM((chips,) + piece, F32),
            pltpu.VMEM((plane,) + piece, F32),
            pltpu.VMEM((Z_LO * narrow,) + piece, F32),
            pltpu.VMEM((chips,) + piece, F32),
            pltpu.SemaphoreType.REGULAR,
            pltpu.SemaphoreType.REGULAR,
            dma((11,)),
            dma,
            dma,
        ]
        + pair(3)
        + pair(ITERS, 6)
        + pair(ITERS, CORES * narrow)
        + pair(ITERS, count)
        + pair(plane)
        + pair(Z_LO * narrow)
        + pair(chips),
        compiler_params=pltpu.CompilerParams(
            collective_id=0, has_side_effects=True, vmem_limit_bytes=61 * 1024 * 1024
        ),
    )(
        local_count,
        remote_count,
        grad_in,
        phi_slope,
        activations,
        weight,
        jnp.transpose(send_list[0]),
        local_tiles[0],
        remote_tiles[0],
        local_rows,
        local_cols,
        remote_rows,
        remote_cols,
    )
    return pl.pallas_call(
        hand_on,
        out_shape=(
            jax.ShapeDtypeStruct((rows, hidden), F32),
            jax.ShapeDtypeStruct((hidden, hidden), F32),
        ),
        in_specs=[vmem] * 2,
        out_specs=(hbm, hbm),
        scratch_shapes=[dma((2,))],
    )(adjoint, weight_grad.reshape(hidden, hidden))


def solution(mesh):
    placed = (
        P(("wide", "narrow"), None),
        P(("wide", "narrow"), None),
        P(("wide", "narrow"), None),
        P(),
        P(("wide", "narrow"), None, None, None),
        P(("wide", "narrow"), None),
        P(("wide", "narrow"), None),
        P(("wide", "narrow")),
        P(("wide", "narrow"), None, None, None),
        P(("wide", "narrow"), None),
        P(("wide", "narrow"), None),
        P(("wide", "narrow")),
        P(("wide", "narrow"), None, None),
    )
    return jax.shard_map(
        per_device,
        mesh=mesh,
        in_specs=placed,
        out_specs=(P(("wide", "narrow"), None), P()),
        check_vma=False,
    )
```

```python
import functools
import math

import jax
import jax.numpy as jnp
from jax import lax
from jax.experimental import pallas as pl
from jax.experimental.pallas import tpu as pltpu
from jax.sharding import PartitionSpec as P

ITERS = 2
GAMMA = 0.5
Z_LO = 4
CORES = 2
MESH = pl.DeviceIdType.MESH
F32 = jnp.float32
BF16 = jnp.bfloat16


def loop(count, body, start=0):
    def step(i, carry):
        body(i)
        return carry

    lax.fori_loop(start, count, step, 0)


def kernel(
    cfg,
    local_count,
    remote_count,
    grad_hbm,
    phi_hbm,
    act_hbm,
    weight_hbm,
    list_hbm,
    local_hbm,
    remote_hbm,
    local_rows,
    local_cols,
    remote_rows,
    remote_cols,
    adj_hbm,
    wg_ref,
    adj_ref,
    grad_ref,
    phi_ref,
    act_ref,
    weight_ref,
    list_ref,
    tiles,
    local_at,
    remote_at,
    slot_rows,
    slot_of,
    table,
    lists,
    index,
    picked,
    send,
    halo,
    total,
    part,
    plane_sum,
    column_sum,
    wg_all,
    know_plane,
    know_space,
    in_sem,
    slot_sem,
    out_sem,
    list_send,
    list_recv,
    group_send,
    group_recv,
    twin_send,
    twin_recv,
    swap_send,
    swap_recv,
    plane_send,
    plane_recv,
    column_send,
    column_recv,
    last_send,
    last_recv,
):
    plane, narrow, rows, tb, sendn, batch, scale = cfg
    depth = Z_LO * narrow
    chips = plane // CORES
    side = math.isqrt(chips)
    count = Z_LO * chips
    per_chip = CORES * sendn
    hidden = grad_ref.shape[1]
    n_local, n_remote = local_hbm.shape[0], remote_hbm.shape[0]
    zero_slot = n_local + n_remote
    blocks = rows // tb
    group_rows = narrow * rows
    group_blocks = narrow * blocks
    layer_blocks = chips * per_chip // tb
    halo_blocks = Z_LO * layer_blocks
    span = math.gcd(layer_blocks, 7)

    wide_at, m = lax.axis_index("wide"), lax.axis_index("narrow")
    low, me = wide_at // plane, lax.rem(wide_at, plane)
    z = m * Z_LO + low
    core, chip = lax.rem(me, CORES), me // CORES
    twin = me + 1 - 2 * core
    even = lax.rem(low, 2) == 0

    def device(z_at, in_plane):
        return (lax.rem(z_at, Z_LO) * plane + in_plane, z_at // Z_LO)

    def offset(k):
        phase, inner = k // (count // 2), lax.rem(k, count // 2)
        turn, j = lax.rem(inner, 2), inner // 2
        i_x = j // side
        i_y = lax.rem(j, side)

        def far_first(i):
            if side == 1:
                return 0 * i
            return jnp.where(i == 0, 2, jnp.where(i == 1, 1, jnp.where(i == 2, 3, 0)))

        dx, dy = far_first(i_x), far_first(i_y)
        dx, dy = jnp.where(core == 0, dx, dy), jnp.where(core == 0, dy, dx)
        dx = jnp.where(turn == 0, dx, lax.rem(side - dx, side))
        dy = jnp.where(turn == 0, dy, lax.rem(side - dy, side))
        two = jnp.where(even, 2, depth - 2)
        dz = jnp.where(phase == 0, jnp.where(turn == 0, two, 0), jnp.where(turn == 0, 1, depth - 1))
        return dz, dx, dy

    self_k = count // 2 - 1

    def target(k):
        dz, dx, dy = offset(k)
        return lax.rem(z + dz, depth), lax.rem(chip // side + dx, side) * side + lax.rem(lax.rem(chip, side) + dy, side)

    def partners(body):
        loop(self_k, body)
        loop(count, body, self_k + 1)

    barrier = pltpu.get_barrier_semaphore()

    def greet(where):
        pl.semaphore_signal(barrier, inc=1, device_id=where, device_id_type=MESH)

    x, y = chip // side, lax.rem(chip, side)
    x_line = [device(z, (lax.rem(x + k, side) * side + y) * CORES + core) for k in range(1, side)]
    y_line = [device(z, (x * side + lax.rem(y + k, side)) * CORES + core) for k in range(1, side)]
    z_line = [device(lax.rem(z + k, depth), me) for k in (1, 2, depth - 2, depth - 1)]
    group = [device(lax.rem(z + Z_LO * k, depth), me) for k in range(1, narrow)]
    first_round = z_line + group + x_line + y_line + [device(z, twin)]
    for where in first_round:
        greet(where)

    def tell(semaphore, listeners):
        for where in listeners:
            pl.semaphore_signal(semaphore, inc=1, device_id=where, device_id_type=MESH)
        if listeners:
            pl.semaphore_wait(semaphore, len(listeners))

    inputs = [
        (grad_hbm, grad_ref),
        (phi_hbm, phi_ref),
        (weight_hbm, weight_ref),
        (list_hbm, list_ref),
        (local_rows, local_at.at[0:1]),
        (local_cols, local_at.at[1:2]),
        (remote_rows, remote_at.at[0:1]),
        (remote_cols, remote_at.at[1:2]),
        (local_hbm, tiles.at[pl.ds(0, n_local)]),
        (remote_hbm, tiles.at[pl.ds(n_local, n_remote)]),
        (act_hbm, act_ref),
    ]
    inputs = [pltpu.make_async_copy(src, dst, in_sem.at[i]) for i, (src, dst) in enumerate(inputs)]
    for copy in inputs:
        copy.start()

    def make_message(it, adjoint):
        mapped = lax.dot_general(
            adjoint.astype(BF16), weight_ref[...], (((1,), (1,)), ((), ())), preferred_element_type=F32
        )
        message = (mapped * phi_ref[...].astype(F32)).astype(BF16)
        table[it, core, pl.ds(pl.multiple_of(m * rows, rows), rows), :] = message

    for copy in inputs[:3]:
        copy.wait()
    make_message(0, grad_ref[...])
    pl.semaphore_wait(barrier, len(first_round))

    half = rows // 2

    def group_half(it, k, piece):
        at = pl.multiple_of(lax.rem(m + narrow - k, narrow) * rows + piece * half, half)
        return table.at[it, core, pl.ds(at, half)]

    hops = ((1, 0, 0), (-1, 0, 1), (1, 0, 1), (-1, 0, 0), (1, 1, 0), (-1, narrow - 1, 1))

    def group_copy(it, i):
        way, k, piece = hops[i]
        ref = group_half(it, k, piece)
        return pltpu.make_async_remote_copy(
            src_ref=ref,
            dst_ref=ref,
            send_sem=group_send.at[it, i],
            recv_sem=group_recv.at[it, i],
            device_id=device(lax.rem(z + depth + way * Z_LO, depth), me),
            device_id_type=MESH,
        )

    def twin_copy(it, k, piece):
        ref = group_half(it, k, piece)
        return pltpu.make_async_remote_copy(
            src_ref=ref,
            dst_ref=ref,
            send_sem=twin_send.at[it, CORES * k + piece],
            recv_sem=twin_recv.at[it, CORES * k + piece],
            device_id=device(z, twin),
            device_id_type=MESH,
        )

    away = jnp.where(low < Z_LO // 2, Z_LO - 1, 0)
    holder = lax.rem(z + jnp.where(low < Z_LO // 2, Z_LO, depth - Z_LO), depth)

    def list_copy(i):
        src, kind, where = (
            (list_ref, 1, device(holder, me)),
            (list_ref, 0, device(z, twin)),
            (lists.at[1, core], 1, device(z, twin)),
        )[i]
        return pltpu.make_async_remote_copy(
            src_ref=src,
            dst_ref=lists.at[kind, core],
            send_sem=list_send.at[i],
            recv_sem=list_recv.at[i],
            device_id=where,
            device_id_type=MESH,
        )

    def make_index(g):
        lane = lax.broadcasted_iota(jnp.int32, (sendn, Z_LO * plane), 1)
        is_away = (lane >= away * plane) & (lane < (away + 1) * plane)
        merged = jnp.where(is_away, lists[1, g], lists[0, g])
        merged = jnp.where(core == 0, merged, pltpu.roll(merged, Z_LO * plane - 1, 1))
        for c in range(count):
            at = c * CORES
            index[c, g * sendn : (g + 1) * sendn, :] = jnp.broadcast_to(merged[:, at : at + 1], (sendn, 128))

    def make_slots():
        def row_of(at, alive, per_row, first):
            key = at[0:1] * per_row + at[1:2]
            slot = lax.broadcasted_iota(jnp.int32, key.shape, 1)
            key = jnp.where(slot < alive, key, -1)
            wide_key = jnp.broadcast_to(key, (128, key.shape[1]))
            pair = lax.broadcasted_iota(jnp.int32, wide_key.shape, 0)
            value = lax.broadcasted_iota(jnp.int32, wide_key.shape, 1) + (first - zero_slot)
            found = zero_slot + jnp.sum(jnp.where(wide_key == pair, value, 0), axis=1, keepdims=True)
            return jnp.transpose(jnp.broadcast_to(found, (128, 128)))[0:1]

        slot_rows[0:1] = row_of(local_at[...], local_count[0], group_blocks, 0)
        slot_rows[1:2] = row_of(remote_at[...], remote_count[0], halo_blocks, n_local)
        copy = pltpu.make_async_copy(slot_rows, slot_of, slot_sem)
        copy.start()
        copy.wait()

    my_rows = pl.ds(pl.multiple_of((low * chips + chip) * per_chip, 16), per_chip)

    def swap_copy(it, k):
        z_at, chip_at = target(k)
        return pltpu.make_async_remote_copy(
            src_ref=send.at[it, k],
            dst_ref=halo.at[it, my_rows],
            send_sem=swap_send.at[it, k],
            recv_sem=swap_recv.at[it, k],
            device_id=device(z_at, chip_at * CORES + core),
            device_id_type=MESH,
        )

    batches = count // batch
    early = batches // 2

    def select(it, c, g):
        wanted = []
        for j in range(batch):
            z_at, chip_at = target(c * batch + j)
            wanted.append(lax.rem(z_at, Z_LO) * chips + chip_at)
        g_rows = pl.ds(pl.multiple_of(g * sendn, 8), sendn)
        want = jnp.concatenate([index[w, g_rows, :] for w in wanted], axis=0)
        lane = lax.broadcasted_iota(jnp.int32, want.shape, 1)
        hot = jnp.concatenate(
            [jnp.where(want == lane + at, 1.0, 0.0).astype(BF16) for at in range(0, group_rows, 128)], axis=1
        )
        got = jnp.dot(hot, table[it, g], preferred_element_type=F32)
        for j in range(batch):
            picked[c, j, g_rows, :] = got[j * sendn : (j + 1) * sendn]

    def send_batch(it, c):
        def post(j):
            k = c * batch + j
            send[it, k] = picked[c, j].astype(BF16)

            @pl.when(k != self_k)
            def _():
                swap_copy(it, k).start()

        select(it, c, 1 - core)
        loop(batch, post)

    def both_then_send(it, c):
        select(it, c, core)
        send_batch(it, c)

    def tile_rows(kind, per_row, first, width):
        return jnp.concatenate(
            [
                jnp.concatenate([tiles[slot_of[kind, r * per_row + first + c]] for c in range(width)], axis=1)
                for r in range(blocks)
            ],
            axis=0,
        )

    def gather_group(it):
        for i in range(4):
            group_copy(it, i).start()
        for piece in range(2):
            twin_copy(it, 0, piece).start()

        @pl.when(it == 0)
        def _():
            inputs[3].wait()
            list_copy(0).start()
            list_copy(1).start()
            lists[0, core] = list_ref[...]
            tell(know_plane, x_line)
            tell(know_space, z_line + [device(z, twin)])

        for i in range(2):
            group_copy(it, i).wait_recv()
            group_copy(it, i + 4).start()

        @pl.when(it == 0)
        def _():
            for copy in inputs[4:8]:
                copy.wait()
            tiles[zero_slot] = jnp.zeros((tb, tb), BF16)
            make_slots()
            list_copy(0).wait_recv()
            list_copy(2).start()
            list_copy(1).wait_recv()
            list_copy(2).wait_recv()
            for g in range(CORES):
                make_index(g)
            for i in range(3):
                list_copy(i).wait_send()
            for copy in inputs[8:10]:
                copy.wait()

        for i, (way, k, piece) in enumerate(hops):
            if i > 1:
                group_copy(it, i).wait_recv()
            twin_copy(it, (k + narrow + way) % narrow, piece).start()

        loop(early, lambda c: select(it, c, core))
        total[...] = jnp.dot(
            tile_rows(0, group_blocks, 0, group_blocks), table[it, core], preferred_element_type=F32
        )
        for k in range(narrow):
            for piece in range(2):
                twin_copy(it, k, piece).wait_recv()

    def layer(it, b):
        def some(i):
            first = b * layer_blocks + i * span
            source = halo[it, pl.ds(pl.multiple_of(first * tb, tb), span * tb), :]
            total[...] += jnp.dot(tile_rows(1, halo_blocks, first, span), source, preferred_element_type=F32)

        loop(layer_blocks // span, some)

    def iterate(it):
        gather_group(it)
        loop(early, lambda c: send_batch(it, c))
        loop(batches, lambda c: both_then_send(it, c), early)
        halo[it, my_rows, :] = send[it, self_k]
        arrived = lambda k: swap_copy(it, k).wait_recv()
        loop(self_k, arrived)
        layer(it, low)
        layer(it, lax.rem(low + 2, Z_LO))
        loop(count, arrived, self_k + 1)
        last = layer_blocks // span

        def piece(i):
            first = lax.rem(low + 1 + 2 * (i // last), Z_LO) * layer_blocks + i % last * span
            source = halo[it, pl.ds(pl.multiple_of(first * tb, tb), span * tb), :]
            return jnp.dot(tile_rows(1, halo_blocks, first, span), source, preferred_element_type=F32)

        far = piece(0)
        for i in range(1, 2 * last):
            far += piece(i)
        adj_ref[...] = grad_ref[...] + GAMMA * (total[...] + far)

        @pl.when(it < ITERS - 1)
        def _():
            make_message(it + 1, adj_ref[...])

    loop(ITERS, iterate)
    adj_copy = pltpu.make_async_copy(adj_ref, adj_hbm, out_sem)
    adj_copy.start()

    inputs[10].wait()
    gradient = lax.dot_general(
        act_ref[...], adj_ref[...].astype(BF16), (((0,), (0,)), ((), ())), preferred_element_type=F32
    )
    piece_rows = hidden // chips
    for j in range(chips):
        part[j] = gradient[j * piece_rows : (j + 1) * piece_rows]

    def share(src, dst, sems, k, where):
        return pltpu.make_async_remote_copy(
            src_ref=src, dst_ref=dst, send_sem=sems[0].at[k], recv_sem=sems[1].at[k], device_id=where, device_id_type=MESH
        )

    def chip_ahead(k):
        return lax.rem(chip + k, chips)

    def plane_copy(k):
        other = lax.rem(me + k, plane)
        return share(part.at[other // CORES], plane_sum.at[me], (plane_send, plane_recv), k, device(z, other))

    loop(plane - 1, lambda i: plane_copy(lax.rem(i + 3 * plane // 8, plane - 1) + 1).start())
    plane_sum[me] = part[chip]
    loop(plane, lambda k: plane_copy(k).wait_recv(), 1)
    column_sum[z] = jnp.sum(plane_sum[...], axis=0)

    def column_copy(k):
        where = device(lax.rem(z + k, depth), me)
        return share(column_sum.at[z], column_sum.at[z], (column_send, column_recv), k, where)

    for k in sorted(range(1, depth), key=lambda k: -min(k, depth - k)):
        column_copy(k).start()
    loop(depth, lambda k: column_copy(k).wait_recv(), 1)
    wg_all[chip] = jnp.sum(column_sum[...], axis=0) * scale

    def last_copy(k):
        where = device(z, chip_ahead(k) * CORES + core)
        return share(wg_all.at[chip], wg_all.at[chip], (last_send, last_recv), k, where)

    if chips > 1:
        loop(chips - 1, lambda i: last_copy(lax.rem(i + 5 * chips // 16, chips - 1) + 1).start())
    loop(chips, lambda k: last_copy(k).wait_recv(), 1)
    wg_ref[...] = wg_all[...]
    loop(plane, lambda k: plane_copy(k).wait_send(), 1)
    loop(depth, lambda k: column_copy(k).wait_send(), 1)
    loop(chips, lambda k: last_copy(k).wait_send(), 1)
    adj_copy.wait()

    def sent(it):
        for i in range(len(hops)):
            group_copy(it, i).wait_send()
        for k in range(narrow):
            for piece in range(2):
                twin_copy(it, k, piece).wait_send()
        partners(lambda k: swap_copy(it, k).wait_send())

    loop(ITERS, sent)


def hand_on(adj_src, wg_src, adj_dst, wg_dst, sems):
    copies = [
        pltpu.make_async_copy(adj_src, adj_dst, sems.at[0]),
        pltpu.make_async_copy(wg_src, wg_dst, sems.at[1]),
    ]
    for copy in copies:
        copy.start()
    for copy in copies:
        copy.wait()


def per_device(
    grad_in,
    phi_slope,
    activations,
    weight,
    local_tiles,
    local_rows,
    local_cols,
    local_count,
    remote_tiles,
    remote_rows,
    remote_cols,
    remote_count,
    send_list,
):
    wide, narrow = lax.axis_size("wide"), lax.axis_size("narrow")
    plane = wide // Z_LO
    chips = plane // CORES
    rows, hidden = grad_in.shape
    tb = local_tiles.shape[2]
    sendn = send_list.shape[2]
    n_local, n_remote = local_tiles.shape[1], remote_tiles.shape[1]
    count = Z_LO * chips
    batch = math.gcd(count // 2, 8)
    scale = GAMMA / math.sqrt(rows * wide * narrow)
    vmem = pl.BlockSpec(memory_space=pltpu.VMEM)
    hbm = pl.BlockSpec(memory_space=pltpu.HBM)
    smem = pl.BlockSpec(memory_space=pltpu.SMEM)
    piece = (hidden // chips, hidden)
    dma = pltpu.SemaphoreType.DMA
    pair = lambda *shape: [dma(shape), dma(shape)]
    adjoint, weight_grad = pl.pallas_call(
        functools.partial(kernel, (plane, narrow, rows, tb, sendn, batch, scale)),
        out_shape=(
            jax.ShapeDtypeStruct((rows, hidden), F32),
            jax.ShapeDtypeStruct((chips,) + piece, F32),
        ),
        in_specs=[smem] * 2 + [hbm] * 11,
        out_specs=(hbm, vmem),
        scratch_shapes=[
            pltpu.VMEM((rows, hidden), F32),
            pltpu.VMEM((rows, hidden), F32),
            pltpu.VMEM((rows, hidden), BF16),
            pltpu.VMEM((rows, hidden), BF16),
            pltpu.VMEM((hidden, hidden), BF16),
            pltpu.VMEM((sendn, wide), jnp.int32),
            pltpu.VMEM((n_local + n_remote + 1, tb, tb), BF16),
            pltpu.VMEM((2, n_local), jnp.int32),
            pltpu.VMEM((2, n_remote), jnp.int32),
            pltpu.VMEM((8, 128), jnp.int32),
            pltpu.SMEM((8, 128), jnp.int32),
            pltpu.VMEM((ITERS, CORES, narrow * rows, hidden), BF16),
            pltpu.VMEM((2, CORES, sendn, wide), jnp.int32),
            pltpu.VMEM((count, CORES * sendn, 128), jnp.int32),
            pltpu.VMEM((count // batch, batch, CORES * sendn, hidden), F32),
            pltpu.VMEM((ITERS, count, CORES * sendn, hidden), BF16),
            pltpu.VMEM((ITERS, wide * sendn, hidden), BF16),
            pltpu.VMEM((rows, hidden), F32),
            pltpu.VMEM((chips,) + piece, F32),
            pltpu.VMEM((plane,) + piece, F32),
            pltpu.VMEM((Z_LO * narrow,) + piece, F32),
            pltpu.VMEM((chips,) + piece, F32),
            pltpu.SemaphoreType.REGULAR,
            pltpu.SemaphoreType.REGULAR,
            dma((11,)),
            dma,
            dma,
        ]
        + pair(3)
        + pair(ITERS, 6)
        + pair(ITERS, CORES * narrow)
        + pair(ITERS, count)
        + pair(plane)
        + pair(Z_LO * narrow)
        + pair(chips),
        compiler_params=pltpu.CompilerParams(
            collective_id=0, has_side_effects=True, vmem_limit_bytes=61 * 1024 * 1024
        ),
    )(
        local_count,
        remote_count,
        grad_in,
        phi_slope,
        activations,
        weight,
        jnp.transpose(send_list[0]),
        local_tiles[0],
        remote_tiles[0],
        local_rows,
        local_cols,
        remote_rows,
        remote_cols,
    )
    return pl.pallas_call(
        hand_on,
        out_shape=(
            jax.ShapeDtypeStruct((rows, hidden), F32),
            jax.ShapeDtypeStruct((hidden, hidden), F32),
        ),
        in_specs=[vmem] * 2,
        out_specs=(hbm, hbm),
        scratch_shapes=[dma((2,))],
    )(adjoint, weight_grad.reshape(hidden, hidden))


def solution(mesh):
    placed = (
        P(("wide", "narrow"), None),
        P(("wide", "narrow"), None),
        P(("wide", "narrow"), None),
        P(),
        P(("wide", "narrow"), None, None, None),
        P(("wide", "narrow"), None),
        P(("wide", "narrow"), None),
        P(("wide", "narrow")),
        P(("wide", "narrow"), None, None, None),
        P(("wide", "narrow"), None),
        P(("wide", "narrow"), None),
        P(("wide", "narrow")),
        P(("wide", "narrow"), None, None),
    )
    return jax.shard_map(
        per_device,
        mesh=mesh,
        in_specs=placed,
        out_specs=(P(("wide", "narrow"), None), P()),
        check_vma=False,
    )
```
